32 devices in a mesh: dp: 8 (over y, x, core), tensor: 4 (over z).
Axes of the slice: x: 2, y: 2, z: 4, core: 2. Of those that a mesh axis runs over, the one named last changes fastest.
Arguments:
- kept_input: bfloat16 [768, 4096], P(('dp', 'tensor')), may hold values from -6 to 6
- kept_grad: bfloat16 [768, 4096], P(('dp', 'tensor')), may hold values from -6 to 6
- up_weight_t: bfloat16 [8256, 4096], P('tensor'), may hold values from -0.09375 to 0.09375
- up_bias: bfloat16 [8256], P('tensor'), may hold values from -4 to 4
- down_weight: bfloat16 [8256, 4096], P('tensor'), may hold values from -0.0625 to 0.0625
- kept_count: int32 [32], P(('dp', 'tensor')), may hold values from 8 to 24, as said below
Outputs:
- grad_kept: bfloat16 [768, 4096], P(('dp', 'tensor'))
The draws below stay inside these ranges and needn't reach their ends.
Inputs may be any that keep to these rules, and one draw needn't show every extreme that they name: `kept_count`: every block keeps at least 8 and at most 24 of its 24 slots, some block exactly 24. Among the 8 blocks of one tensor index taken in order of g, the blocks before block g keep g * 16 + e tokens together with e between -4 and 4, and e is 0 for g = 0 and for g = 8 (all 8 blocks together keep exactly 128 tokens).
All inputs are finite; a program needn't handle non-finite values.
Results may differ from the reference program's by a relative error of at most 0.014.
Values may be sent and summed in bfloat16 or wider, within the bound.
A program may use at most 64 MiB of HBM per device.

```python
import jax
import jax.numpy as jnp
from jax import lax

D = 4096
FF = 8256
BAL = 16
KEPT_ROWS = 768
N_DP = 8
N_TENSOR = 4


def draw_kept_count(key, part):
    halo_width = BAL // 4
    key_excess, key_pick = jax.random.split(key, 2)
    inner = jax.random.randint(key_excess, (N_DP - 1, N_TENSOR), -halo_width, halo_width + 1)
    chosen = jax.random.randint(key_pick, (1, N_TENSOR), 1, N_DP - 1)
    positions = jnp.arange(1, N_DP, dtype=jnp.int32)[:, None]
    inner = jnp.where(positions == chosen, -halo_width, inner)
    inner = jnp.where(positions == chosen + 1, halo_width, inner)
    border = jnp.zeros((1, N_TENSOR), jnp.int32)
    excess = jnp.concatenate((border, inner.astype(jnp.int32), border), axis=0)
    counts = BAL + excess[1:] - excess[:-1]
    return counts.reshape(-1).astype(jnp.int32)


def steps_of(rng, shape, shards, least, high):
    loudness = 1.0
    for position, shards_of in shards:
        steps = jax.random.uniform(jax.random.fold_in(jax.random.fold_in(rng, 6), position), (shards_of,), jnp.float32, least / len(shards), high / len(shards))
        loudness = loudness * jnp.repeat(jnp.exp(steps), shape[position] // shards_of).reshape((-1,) + (1,) * (len(shape) - 1 - position))
    return loudness


def noise(rng, shape, scale, bound, shards=(), held_as=jnp.bfloat16):
    loudness = steps_of(rng, shape, shards, -0.22, 0.18) if shards else 1.0
    array = jax.random.normal(rng, shape, jnp.float32) * scale * loudness
    return jnp.minimum(jnp.maximum(array, -bound), bound).astype(held_as)


def setup_inputs(seed: int = 0) -> dict:
    key_list = jax.random.split(jax.random.key(seed), 7)
    kept_input = noise(key_list[0], (KEPT_ROWS, D), 1.0, 6.0, ((0, 32),))
    kept_grad = noise(key_list[1], (KEPT_ROWS, D), 1.0, 6.0, ((0, 32),))
    up_weight_t = noise(key_list[2], (FF, D), D ** -0.5, 0.09375, ((0, 4),))
    up_bias = noise(key_list[3], (FF,), 1.0, 4.0, ((0, 4),))
    down_weight = noise(key_list[4], (FF, D), FF ** -0.5, 0.0625, ((0, 4),))
    kept_count = draw_kept_count(jax.random.fold_in(key_list[6], 71), 0)
    return dict(kept_input=kept_input, kept_grad=kept_grad, up_weight_t=up_weight_t, up_bias=up_bias, down_weight=down_weight, kept_count=kept_count)


INV_SQRT_TWO = 0.7071067811865476
INV_SQRT_TWO_PI = 0.3989422804014327


def gelu_slope(values):
    return 0.5 * (1.0 + lax.erf(values * INV_SQRT_TWO)) + values * jnp.exp(-0.5 * values * values) * INV_SQRT_TWO_PI


def reference(kept_input, kept_grad, up_weight_t, up_bias, down_weight, kept_count):
    blocks = kept_count.shape[0]
    slots = kept_input.shape[0] // blocks
    live = jnp.arange(slots, dtype=jnp.int32)[None, :] < kept_count[:, None]
    kept_total = N_DP * N_TENSOR * BAL
    row_ids = jnp.nonzero(live.reshape(-1), size=kept_total)[0].astype(jnp.int32)
    inputs = kept_input[row_ids]
    out_grads = kept_grad[row_ids]
    block_width = FF // N_TENSOR

    def block_term(summed, tensor_rank):
        first_row = tensor_rank * block_width
        up_block = lax.dynamic_slice_in_dim(up_weight_t, first_row, block_width, 0)
        bias_block = lax.dynamic_slice_in_dim(up_bias, first_row, block_width, 0)
        down_block = lax.dynamic_slice_in_dim(down_weight, first_row, block_width, 0)
        preact = jnp.dot(inputs, up_block.T, preferred_element_type=jnp.float32) + bias_block.astype(jnp.float32)
        down_grad = jnp.dot(out_grads, down_block.T, preferred_element_type=jnp.float32)
        pre_grad = (gelu_slope(preact) * down_grad).astype(jnp.bfloat16)
        rounded = jnp.dot(pre_grad, up_block, preferred_element_type=jnp.float32).astype(jnp.bfloat16)
        rounded = lax.optimization_barrier(rounded)
        return summed + rounded.astype(jnp.float32), None

    summed, _ = lax.scan(block_term, jnp.zeros((kept_total, D), jnp.float32), jnp.arange(N_TENSOR, dtype=jnp.int32))
    branch = summed.astype(jnp.bfloat16)
    spread = jnp.zeros(kept_input.shape, jnp.float32).at[row_ids].add(branch.astype(jnp.float32))
    result = jnp.where(live.reshape(-1)[:, None], kept_grad.astype(jnp.float32) + spread, jnp.float32(0.0))
    return result.astype(jnp.bfloat16)
```

```python
import functools

import jax
import jax.numpy as jnp
from jax import lax
from jax.experimental import pallas as pl
from jax.experimental.pallas import tpu as pltpu
from jax.sharding import PartitionSpec as P

BAL = 16


INV_SQRT_TWO = 0.7071067811865476
INV_SQRT_TWO_PI = 0.3989422804014327


def prefix(shard, axis, combine, identity):
    length, index = (lax.axis_size(axis), lax.axis_index(axis))
    everything = lax.all_gather(shard, axis)
    start = jnp.broadcast_to(jnp.asarray(identity, shard.dtype), shard.shape)

    def lap(k, before):
        reached = k < index
        new = combine(before, everything[k])
        return jnp.where(reached, new, before)

    return lax.fori_loop(0, length, lap, start)


def padded(block, sides, width):
    for axis, dim in sides:
        count = lax.axis_size(axis)
        forward = [(i, i + 1) for i in range(count - 1)]
        backward = [(target, source) for source, target in forward]
        low = lax.ppermute(
            lax.slice_in_dim(block, block.shape[dim] - width, None, axis=dim), axis, forward
        )
        high = lax.ppermute(lax.slice_in_dim(block, 0, width, axis=dim), axis, backward)
        block = jnp.concatenate([low, block, high], axis=dim)
    return block


def gelu_slope(values):
    return (
        0.5 * (1.0 + lax.erf(values * INV_SQRT_TWO))
        + values * jnp.exp(-0.5 * values * values) * INV_SQRT_TWO_PI
    )


def add_counts(earlier, later):
    return earlier + later


def ffn_rows(stacked, up_weight_t, up_bias, down_weight):
    contract = (((1,), (1,)), ((), ()))
    bias_wide = up_bias.astype(jnp.float32)
    piece_rows = lax.all_gather(stacked, "tensor", axis=0, tiled=True)
    inputs = piece_rows[:, 0]
    out_grads = piece_rows[:, 1]
    preact = (
        lax.dot_general(inputs, up_weight_t, contract, preferred_element_type=jnp.float32)
        + bias_wide
    )
    down_grad = lax.dot_general(
        out_grads, down_weight, contract, preferred_element_type=jnp.float32
    )
    pre_grad = (gelu_slope(preact) * down_grad).astype(jnp.bfloat16)
    partials = jnp.dot(pre_grad, up_weight_t, preferred_element_type=jnp.float32)
    return lax.psum_scatter(
        partials.astype(jnp.bfloat16), "tensor", scatter_dimension=0, tiled=True
    )


def body(kept_input, kept_grad, up_weight_t, up_bias, down_weight, kept_count):
    kmax = kept_input.shape[0]
    count_here = kept_count[0]
    entries = jnp.arange(kmax, dtype=jnp.int32)
    usable = entries < count_here
    stacked = jnp.stack((kept_input, kept_grad), axis=1)
    stacked = jnp.where(usable[:, None, None], stacked, jnp.zeros_like(stacked))
    halo_width = BAL // 4
    spots = BAL + 2 * halo_width
    first_slot = prefix(count_here, "dp", add_counts, jnp.int32(0))
    excess = first_slot - lax.axis_index("dp") * BAL
    target = excess + entries + halo_width
    placing = (target[None, :] == jnp.arange(spots, dtype=jnp.int32)[:, None]) & usable[None, :]
    placing_mat = placing.astype(jnp.bfloat16)
    outgoing = jnp.einsum(
        "sk,kcd->scd", placing_mat, stacked, preferred_element_type=jnp.float32
    ).astype(jnp.bfloat16)
    widened = padded(outgoing, (("dp", 0),), halo_width)
    owned = outgoing[halo_width : halo_width + BAL].astype(jnp.float32)
    owned = owned.at[:halo_width].add(widened[:halo_width].astype(jnp.float32))
    owned = owned.at[BAL - halo_width :].add(
        widened[widened.shape[0] - halo_width :].astype(jnp.float32)
    )
    branch = ffn_rows(owned.astype(jnp.bfloat16), up_weight_t, up_bias, down_weight)
    returned = padded(branch, (("dp", 0),), halo_width)
    own_branch = jnp.einsum(
        "sk,sd->kd", placing_mat, returned, preferred_element_type=jnp.float32
    ).astype(jnp.bfloat16)
    summed = kept_grad.astype(jnp.float32) + own_branch.astype(jnp.float32)
    return jnp.where(usable[:, None], summed, jnp.float32(0.0)).astype(jnp.bfloat16)


ROWS = 16
COLS = 512
VMEM_LIMIT = 58 * 1024 * 1024
MESH = pl.DeviceIdType.MESH
NT = (((1,), (1,)), ((), ()))


def one_hot(shape, picked):
    rows = lax.broadcasted_iota(jnp.int32, shape, 0)
    cols = lax.broadcasted_iota(jnp.int32, shape, 1)
    return picked(rows, cols).astype(jnp.float32).astype(jnp.bfloat16)


def place(matrix, block):
    return jnp.dot(matrix, block, preferred_element_type=jnp.float32)


def fused_kernel(
    n_dp, n_t, x_ref, g_ref, count_ref, bias_ref, up_hbm, down_hbm, out_ref,
    up, down, rows_in, terms, taken, branch, acc_x, acc_g, slopes,
    count_own, counts, halo_out, halo_in, back_out, back_in,
    w_sem, count_send, count_recv, halo_send, halo_recv, back_send, back_recv,
    in_send, in_recv, term_send, term_recv,
):
    me = lax.axis_index("dp")
    t = lax.axis_index("tensor")
    kmax, width = x_ref.shape
    chunks = width // COLS
    halo = BAL // 4
    groups = ROWS // halo
    wide = width // groups
    per_group = wide // COLS
    left = lax.rem(me + n_dp - 1, n_dp)
    right = lax.rem(me + 1, n_dp)

    def weight_copies(c):
        cols = pl.ds(pl.multiple_of(c * COLS, COLS), COLS)
        return (
            pltpu.make_async_copy(up_hbm.at[:, cols], up.at[c], w_sem.at[0, c]),
            pltpu.make_async_copy(down_hbm.at[:, cols], down.at[c], w_sem.at[1, c]),
        )

    @pl.loop(0, chunks)
    def _(c):
        for copy in weight_copies(c):
            copy.start()

    barrier = pltpu.get_barrier_semaphore()
    for k in range(1, n_dp):
        pl.semaphore_signal(
            barrier, inc=1, device_id={"dp": lax.rem(me + k, n_dp)}, device_id_type=MESH
        )
    for k in range(1, n_t):
        pl.semaphore_signal(
            barrier, inc=1, device_id={"tensor": lax.rem(t + k, n_t)}, device_id_type=MESH
        )

    here = count_ref[0]
    count_own[...] = jnp.full(count_own.shape, here, jnp.int32)
    for j in range(groups):
        cols = slice(j * wide, (j + 1) * wide)
        head = one_hot((ROWS, kmax), lambda r, k: (r // halo == j) & (k == r % halo))
        tail = one_hot(
            (ROWS, kmax), lambda r, k: (r // halo == j) & (k == here - halo + r % halo)
        )
        for i, ref in enumerate((x_ref, g_ref)):
            for side, matrix in enumerate((head, tail)):
                part = place(matrix, ref[:, cols]).astype(jnp.bfloat16)
                if j == 0:
                    halo_out[side, i] = part
                else:
                    halo_out[side, i] += part
    pl.semaphore_wait(barrier, n_dp - 1 + n_t - 1)

    def count_copy(k, source):
        return pltpu.make_async_remote_copy(
            src_ref=count_own, dst_ref=counts.at[source],
            send_sem=count_send.at[k - 1], recv_sem=count_recv.at[source],
            device_id={"dp": lax.rem(me + k, n_dp)}, device_id_type=MESH,
        )

    def side_copy(side, source, target, send, recv):
        return pltpu.make_async_remote_copy(
            src_ref=source.at[side], dst_ref=target.at[1 - side],
            send_sem=send.at[side], recv_sem=recv.at[1 - side],
            device_id={"dp": right if side else left}, device_id_type=MESH,
        )

    for side in range(2):
        side_copy(side, halo_out, halo_in, halo_send, halo_recv).start()
    for k in range(1, n_dp):
        count_copy(k, me).start()
    for k in range(1, n_dp):
        count_copy(k, lax.rem(me + n_dp - k, n_dp)).wait_recv()
    before = jnp.zeros(count_own.shape, jnp.int32)
    for j in range(n_dp):
        before = before + jnp.where(j < me, counts[j], 0)
    excess = (before - me * BAL)[0:1, 0:1]
    following = excess + here - BAL

    def in_copy(k, c, source):
        return pltpu.make_async_remote_copy(
            src_ref=rows_in.at[source, c], dst_ref=rows_in.at[source, c],
            send_sem=in_send.at[k - 1, c], recv_sem=in_recv.at[source, c],
            device_id={"tensor": lax.rem(t + k, n_t)}, device_id_type=MESH,
        )

    own_at = one_hot(
        (ROWS, kmax), lambda p, k: (k == p - excess) & (k < here)
    )
    for side in range(2):
        side_copy(side, halo_out, halo_in, halo_send, halo_recv).wait_recv()
    for j in range(groups):
        cols = slice(j * wide, (j + 1) * wide)
        from_left = one_hot(
            (ROWS, ROWS), lambda p, r: (r == j * halo + halo - excess + p) & (p < excess)
        )
        from_right = one_hot(
            (ROWS, ROWS),
            lambda p, r: (r == j * halo + p - BAL - following) & (p >= BAL + following),
        )
        for i, ref in enumerate((x_ref, g_ref)):
            window = (
                place(own_at, ref[:, cols])
                + place(from_left, halo_in[0, i])
                + place(from_right, halo_in[1, i])
            ).astype(jnp.bfloat16)
            for s in range(per_group):
                rows_in[t, j * per_group + s, i] = window[:, s * COLS : (s + 1) * COLS]
        for s in range(per_group):
            for k in range(1, n_t):
                in_copy(k, j * per_group + s, t).start()

    acc_x[...] = jnp.broadcast_to(bias_ref[...].astype(jnp.float32), acc_x.shape)
    acc_g[...] = jnp.zeros_like(acc_g)

    @pl.loop(0, chunks)
    def _(c):
        for copy in weight_copies(c):
            copy.wait()
        for k in range(1, n_t):
            in_copy(k, c, lax.rem(t + n_t - k, n_t)).wait_recv()
        x = rows_in[:, c, 0].reshape(n_t * ROWS, COLS)
        g = rows_in[:, c, 1].reshape(n_t * ROWS, COLS)
        acc_x[...] += lax.dot_general(x, up[c], NT, preferred_element_type=jnp.float32)
        acc_g[...] += lax.dot_general(g, down[c], NT, preferred_element_type=jnp.float32)

    slopes[...] = (gelu_slope(acc_x[...]) * acc_g[...]).astype(jnp.bfloat16)

    def term_copy(k, c, source):
        dest = lax.rem(t + k, n_t)
        return pltpu.make_async_remote_copy(
            src_ref=terms.at[c, dest], dst_ref=taken.at[source, c],
            send_sem=term_send.at[k - 1, c], recv_sem=term_recv.at[source, c],
            device_id={"tensor": dest}, device_id_type=MESH,
        )

    @pl.loop(0, chunks)
    def _(c):
        term = jnp.dot(slopes[...], up[c], preferred_element_type=jnp.float32)
        terms[c] = term.astype(jnp.bfloat16).reshape(n_t, ROWS, COLS)
        for k in range(1, n_t):
            term_copy(k, c, t).start()

    for c in range(chunks):
        total = terms[c, t].astype(jnp.float32)
        for k in range(1, n_t):
            source = lax.rem(t + n_t - k, n_t)
            term_copy(k, c, source).wait_recv()
            total = total + taken[source, c].astype(jnp.float32)
        branch[:, c * COLS : (c + 1) * COLS] = total.astype(jnp.bfloat16)

    for j in range(groups):
        cols = slice(j * wide, (j + 1) * wide)
        head = one_hot((ROWS, ROWS), lambda r, p: (r // halo == j) & (p == r % halo))
        tail = one_hot(
            (ROWS, ROWS), lambda r, p: (r // halo == j) & (p == BAL - halo + r % halo)
        )
        for side, matrix in enumerate((head, tail)):
            part = place(matrix, branch[:, cols]).astype(jnp.bfloat16)
            if j == 0:
                back_out[side] = part
            else:
                back_out[side] += part
    for side in range(2):
        side_copy(side, back_out, back_in, back_send, back_recv).start()
    for side in range(2):
        side_copy(side, back_out, back_in, back_send, back_recv).wait_recv()

    own_back = one_hot((kmax, ROWS), lambda k, p: p == k + excess)
    live = lax.broadcasted_iota(jnp.int32, (kmax, wide), 0) < here
    for j in range(groups):
        cols = slice(j * wide, (j + 1) * wide)
        left_back = one_hot(
            (kmax, ROWS), lambda k, r: (r == j * halo + halo + excess + k) & (k + excess < 0)
        )
        right_back = one_hot(
            (kmax, ROWS),
            lambda k, r: (r == j * halo + excess + k - BAL)
            & (k + excess >= BAL) & (k + excess < BAL + halo),
        )
        got = (
            place(own_back, branch[:, cols])
            + place(left_back, back_in[0])
            + place(right_back, back_in[1])
        )
        summed = g_ref[:, cols].astype(jnp.float32) + got
        out_ref[:, cols] = jnp.where(live, summed, 0.0).astype(jnp.bfloat16)

    for k in range(1, n_dp):
        count_copy(k, me).wait_send()
    for side in range(2):
        side_copy(side, halo_out, halo_in, halo_send, halo_recv).wait_send()
        side_copy(side, back_out, back_in, back_send, back_recv).wait_send()

    @pl.loop(0, chunks)
    def _(c):
        for k in range(1, n_t):
            in_copy(k, c, t).wait_send()
            term_copy(k, c, t).wait_send()


def fused(kept_input, kept_grad, up_weight_t, up_bias, down_weight, kept_count):
    n_dp, n_t = lax.axis_size("dp"), lax.axis_size("tensor")
    kmax, width = kept_input.shape
    hidden = up_weight_t.shape[0]
    chunks = width // COLS
    wide = width // (ROWS // (BAL // 4))
    tokens = n_t * ROWS
    bf16, f32 = jnp.bfloat16, jnp.float32
    vmem = pl.BlockSpec(memory_space=pltpu.VMEM)
    smem = pl.BlockSpec(memory_space=pltpu.SMEM)
    hbm = pl.BlockSpec(memory_space=pl.ANY)
    dma = pltpu.SemaphoreType.DMA
    return pl.pallas_call(
        functools.partial(fused_kernel, n_dp, n_t),
        out_shape=jax.ShapeDtypeStruct((kmax, width), bf16),
        in_specs=[vmem, vmem, smem, vmem, hbm, hbm],
        out_specs=vmem,
        scratch_shapes=[
            pltpu.VMEM((chunks, hidden, COLS), bf16),
            pltpu.VMEM((chunks, hidden, COLS), bf16),
            pltpu.VMEM((n_t, chunks, 2, ROWS, COLS), bf16),
            pltpu.VMEM((chunks, n_t, ROWS, COLS), bf16),
            pltpu.VMEM((n_t, chunks, ROWS, COLS), bf16),
            pltpu.VMEM((ROWS, width), bf16),
            pltpu.VMEM((tokens, hidden), f32),
            pltpu.VMEM((tokens, hidden), f32),
            pltpu.VMEM((tokens, hidden), bf16),
            pltpu.VMEM((8, 128), jnp.int32),
            pltpu.VMEM((n_dp, 8, 128), jnp.int32),
            pltpu.VMEM((2, 2, ROWS, wide), bf16),
            pltpu.VMEM((2, 2, ROWS, wide), bf16),
            pltpu.VMEM((2, ROWS, wide), bf16),
            pltpu.VMEM((2, ROWS, wide), bf16),
            dma((2, chunks)),
            dma((n_dp - 1,)),
            dma((n_dp,)),
            dma((2,)),
            dma((2,)),
            dma((2,)),
            dma((2,)),
            dma((n_t - 1, chunks)),
            dma((n_t, chunks)),
            dma((n_t - 1, chunks)),
            dma((n_t, chunks)),
        ],
        compiler_params=pltpu.CompilerParams(
            collective_id=0, has_side_effects=True, vmem_limit_bytes=VMEM_LIMIT
        ),
    )(kept_input, kept_grad, kept_count, up_bias.reshape(1, hidden), up_weight_t, down_weight)


def fits(mesh, kept_input, up_weight_t):
    hidden = up_weight_t.shape[0] // mesh.shape["tensor"]
    width = up_weight_t.shape[1]
    weights = 2 * hidden * width * 2
    return (
        hidden % ROWS == 0
        and width % (COLS * 4) == 0
        and BAL == ROWS
        and mesh.shape["dp"] > 1
        and mesh.shape["tensor"] > 1
        and weights < VMEM_LIMIT * 3 // 4
    )


def solution(mesh):
    rows = P(("dp", "tensor"), None)
    placed = (rows, rows, P("tensor", None), P("tensor"), P("tensor", None), P(("dp", "tensor")))

    def run(kept_input, kept_grad, up_weight_t, up_bias, down_weight, kept_count):
        chosen = fused if fits(mesh, kept_input, up_weight_t) else body
        return jax.shard_map(
            chosen, mesh=mesh, in_specs=placed, out_specs=rows, check_vma=False
        )(kept_input, kept_grad, up_weight_t, up_bias, down_weight, kept_count)

    return run
```

```python
import functools

import jax
import jax.numpy as jnp
from jax import lax
from jax.experimental import pallas as pl
from jax.experimental.pallas import tpu as pltpu
from jax.sharding import PartitionSpec as P

BAL = 16


INV_SQRT_TWO = 0.7071067811865476
INV_SQRT_TWO_PI = 0.3989422804014327


def prefix(shard, axis, combine, identity):
    length, index = (lax.axis_size(axis), lax.axis_index(axis))
    everything = lax.all_gather(shard, axis)
    start = jnp.broadcast_to(jnp.asarray(identity, shard.dtype), shard.shape)

    def lap(k, before):
        reached = k < index
        new = combine(before, everything[k])
        return jnp.where(reached, new, before)

    return lax.fori_loop(0, length, lap, start)


def padded(block, sides, width):
    for axis, dim in sides:
        count = lax.axis_size(axis)
        forward = [(i, i + 1) for i in range(count - 1)]
        backward = [(target, source) for source, target in forward]
        low = lax.ppermute(
            lax.slice_in_dim(block, block.shape[dim] - width, None, axis=dim), axis, forward
        )
        high = lax.ppermute(lax.slice_in_dim(block, 0, width, axis=dim), axis, backward)
        block = jnp.concatenate([low, block, high], axis=dim)
    return block


def gelu_slope(values):
    return (
        0.5 * (1.0 + lax.erf(values * INV_SQRT_TWO))
        + values * jnp.exp(-0.5 * values * values) * INV_SQRT_TWO_PI
    )


def add_counts(earlier, later):
    return earlier + later


def ffn_rows(stacked, up_weight_t, up_bias, down_weight):
    contract = (((1,), (1,)), ((), ()))
    bias_wide = up_bias.astype(jnp.float32)
    piece_rows = lax.all_gather(stacked, "tensor", axis=0, tiled=True)
    inputs = piece_rows[:, 0]
    out_grads = piece_rows[:, 1]
    preact = (
        lax.dot_general(inputs, up_weight_t, contract, preferred_element_type=jnp.float32)
        + bias_wide
    )
    down_grad = lax.dot_general(
        out_grads, down_weight, contract, preferred_element_type=jnp.float32
    )
    pre_grad = (gelu_slope(preact) * down_grad).astype(jnp.bfloat16)
    partials = jnp.dot(pre_grad, up_weight_t, preferred_element_type=jnp.float32)
    return lax.psum_scatter(
        partials.astype(jnp.bfloat16), "tensor", scatter_dimension=0, tiled=True
    )


def body(kept_input, kept_grad, up_weight_t, up_bias, down_weight, kept_count):
    kmax = kept_input.shape[0]
    count_here = kept_count[0]
    entries = jnp.arange(kmax, dtype=jnp.int32)
    usable = entries < count_here
    stacked = jnp.stack((kept_input, kept_grad), axis=1)
    stacked = jnp.where(usable[:, None, None], stacked, jnp.zeros_like(stacked))
    halo_width = BAL // 4
    spots = BAL + 2 * halo_width
    first_slot = prefix(count_here, "dp", add_counts, jnp.int32(0))
    excess = first_slot - lax.axis_index("dp") * BAL
    target = excess + entries + halo_width
    placing = (target[None, :] == jnp.arange(spots, dtype=jnp.int32)[:, None]) & usable[None, :]
    placing_mat = placing.astype(jnp.bfloat16)
    outgoing = jnp.einsum(
        "sk,kcd->scd", placing_mat, stacked, preferred_element_type=jnp.float32
    ).astype(jnp.bfloat16)
    widened = padded(outgoing, (("dp", 0),), halo_width)
    owned = outgoing[halo_width : halo_width + BAL].astype(jnp.float32)
    owned = owned.at[:halo_width].add(widened[:halo_width].astype(jnp.float32))
    owned = owned.at[BAL - halo_width :].add(
        widened[widened.shape[0] - halo_width :].astype(jnp.float32)
    )
    branch = ffn_rows(owned.astype(jnp.bfloat16), up_weight_t, up_bias, down_weight)
    returned = padded(branch, (("dp", 0),), halo_width)
    own_branch = jnp.einsum(
        "sk,sd->kd", placing_mat, returned, preferred_element_type=jnp.float32
    ).astype(jnp.bfloat16)
    summed = kept_grad.astype(jnp.float32) + own_branch.astype(jnp.float32)
    return jnp.where(usable[:, None], summed, jnp.float32(0.0)).astype(jnp.bfloat16)


ROWS = 16
COLS = 512
VMEM_LIMIT = 58 * 1024 * 1024
MESH = pl.DeviceIdType.MESH
NT = (((1,), (1,)), ((), ()))


def one_hot(shape, picked):
    rows = lax.broadcasted_iota(jnp.int32, shape, 0)
    cols = lax.broadcasted_iota(jnp.int32, shape, 1)
    return picked(rows, cols).astype(jnp.float32).astype(jnp.bfloat16)


def place(matrix, block):
    return jnp.dot(matrix, block, preferred_element_type=jnp.float32)


def fused_kernel(
    n_dp, n_t, x_ref, g_ref, count_ref, bias_ref, up_hbm, down_hbm, out_ref,
    up, down, rows_in, terms, taken, branch, acc, slopes, pre_grad,
    count_own, counts, halo_out, halo_in, back_out, back_in,
    w_sem, count_send, count_recv, halo_send, halo_recv, back_send, back_recv,
    in_send, in_recv, term_send, term_recv,
):
    me = lax.axis_index("dp")
    t = lax.axis_index("tensor")
    kmax, width = x_ref.shape
    halo = BAL // 4
    groups = ROWS // halo
    wide = width // groups
    narrow = wide // groups
    per_group = wide // COLS
    chunks = width // COLS
    steps = 2 * groups
    left = lax.rem(me + n_dp - 1, n_dp)
    right = lax.rem(me + 1, n_dp)

    def weight_copy(i, j):
        source, target = ((up_hbm, up), (down_hbm, down))[i]
        cols = pl.ds(pl.multiple_of(j * wide, wide), wide)
        return pltpu.make_async_copy(source.at[:, cols], target.at[j], w_sem.at[i, j])

    for i in range(2):
        for j in range(groups):
            weight_copy(i, j).start()

    barrier = pltpu.get_barrier_semaphore()
    for k in range(1, n_dp):
        pl.semaphore_signal(
            barrier, inc=1, device_id={"dp": lax.rem(me + k, n_dp)}, device_id_type=MESH
        )
    for k in range(1, n_t):
        pl.semaphore_signal(
            barrier, inc=1, device_id={"tensor": lax.rem(t + k, n_t)}, device_id_type=MESH
        )

    here = count_ref[0]
    count_own[...] = jnp.full(count_own.shape, here, jnp.int32)
    for side in range(2):
        first = (here - halo) if side else 0
        for i, ref in enumerate((x_ref, g_ref)):
            packed = jnp.zeros((ROWS, wide), jnp.float32)
            for j in range(groups):
                picked = one_hot(
                    (ROWS, kmax), lambda r, k: (r // halo == j) & (k == first + r % halo)
                )
                packed = packed + place(picked, ref[:, j * wide : (j + 1) * wide])
            halo_out[side, i] = packed.astype(jnp.bfloat16)
    pl.semaphore_wait(barrier, n_dp - 1 + n_t - 1)

    def count_copy(k, source):
        return pltpu.make_async_remote_copy(
            src_ref=count_own, dst_ref=counts.at[source],
            send_sem=count_send.at[k - 1], recv_sem=count_recv.at[source],
            device_id={"dp": lax.rem(me + k, n_dp)}, device_id_type=MESH,
        )

    def halo_copy(side, i):
        return pltpu.make_async_remote_copy(
            src_ref=halo_out.at[side, i], dst_ref=halo_in.at[1 - side, i],
            send_sem=halo_send.at[side, i], recv_sem=halo_recv.at[1 - side, i],
            device_id={"dp": right if side else left}, device_id_type=MESH,
        )

    def back_copy(side, j):
        return pltpu.make_async_remote_copy(
            src_ref=back_out.at[side, j], dst_ref=back_in.at[1 - side, j],
            send_sem=back_send.at[side, j], recv_sem=back_recv.at[1 - side, j],
            device_id={"dp": right if side else left}, device_id_type=MESH,
        )

    for k in range(1, n_dp):
        count_copy(k, me).start()
    for i in range(2):
        for side in range(2):
            halo_copy(side, i).start()
    for k in range(1, n_dp):
        count_copy(k, lax.rem(me + n_dp - k, n_dp)).wait_recv()
    before = jnp.zeros(count_own.shape, jnp.int32)
    for j in range(n_dp):
        before = before + jnp.where(j < me, counts[j], 0)
    excess = (before - me * BAL)[0:1, 0:1]
    following = excess + here - BAL

    def in_copy(up_line, source, step):
        return pltpu.make_async_remote_copy(
            src_ref=rows_in.at[source, step], dst_ref=rows_in.at[source, step],
            send_sem=in_send.at[up_line, source, step], recv_sem=in_recv.at[source, step],
            device_id={"tensor": t + 1 if up_line else t - 1}, device_id_type=MESH,
        )

    def pass_on(source, step, up_line, down_line):
        if up_line:
            @pl.when(t < n_t - 1)
            def _():
                in_copy(1, source, step).start()
        if down_line:
            @pl.when(t > 0)
            def _():
                in_copy(0, source, step).start()

    own_at = one_hot((ROWS, kmax), lambda p, k: (k == p - excess) & (k < here))
    from_left, from_right = [], []
    for j in range(groups):
        from_left.append(one_hot(
            (ROWS, ROWS), lambda p, r: (r == j * halo + halo - excess + p) & (p < excess)
        ))
        from_right.append(one_hot(
            (ROWS, ROWS),
            lambda p, r: (r == j * halo + p - BAL - following) & (p >= BAL + following),
        ))
    for i, ref in enumerate((x_ref, g_ref)):
        for side in range(2):
            halo_copy(side, i).wait_recv()
        for j in range(groups):
            rows_in[t, i * groups + j] = (
                place(own_at, ref[:, j * wide : (j + 1) * wide])
                + place(from_left[j], halo_in[0, i])
                + place(from_right[j], halo_in[1, i])
            ).astype(jnp.bfloat16)
            pass_on(t, i * groups + j, True, True)

    def multiply(i, weights, first):
        acc[...] = first

        @pl.loop(0, groups)
        def _(j):
            step = i * groups + j
            for d in range(1, n_t):
                @pl.when(t - d >= 0)
                def _():
                    in_copy(1, t - d, step).wait_recv()
                    pass_on(t - d, step, True, False)

                @pl.when(t + d < n_t)
                def _():
                    in_copy(0, t + d, step).wait_recv()
                    pass_on(t + d, step, False, True)
            weight_copy(i, j).wait()
            block = rows_in[:, step].reshape(n_t * ROWS, wide)
            acc[...] += lax.dot_general(
                block, weights[j], NT, preferred_element_type=jnp.float32
            )

    bias = bias_ref[...].astype(jnp.float32).reshape(1, acc.shape[1])
    multiply(0, up, jnp.broadcast_to(bias, acc.shape))
    slopes[...] = gelu_slope(acc[...])
    multiply(1, down, jnp.zeros(acc.shape, jnp.float32))
    pre_grad[...] = (slopes[...] * acc[...]).astype(jnp.bfloat16)

    def term_copy(k, c, source):
        dest = lax.rem(t + k, n_t)
        return pltpu.make_async_remote_copy(
            src_ref=terms.at[c, dest], dst_ref=taken.at[source, c],
            send_sem=term_send.at[k - 1, c], recv_sem=term_recv.at[source, c],
            device_id={"tensor": dest}, device_id_type=MESH,
        )

    @pl.loop(0, groups)
    def _(j):
        for s in range(per_group):
            c = j * per_group + s
            term = jnp.dot(
                pre_grad[...], up[j, :, s * COLS : (s + 1) * COLS],
                preferred_element_type=jnp.float32,
            )
            terms[c] = term.astype(jnp.bfloat16).reshape(n_t, ROWS, COLS)
            for k in range(1, n_t):
                term_copy(k, c, t).start()

    for j in range(groups):
        for s in range(per_group):
            c = j * per_group + s
            total = terms[c, t].astype(jnp.float32)
            for k in range(1, n_t):
                source = lax.rem(t + n_t - k, n_t)
                term_copy(k, c, source).wait_recv()
                total = total + taken[source, c].astype(jnp.float32)
            branch[:, c * COLS : (c + 1) * COLS] = total.astype(jnp.bfloat16)
        for side in range(2):
            first = (BAL - halo) if side else 0
            packed = jnp.zeros((ROWS, narrow), jnp.float32)
            for q in range(groups):
                picked = one_hot(
                    (ROWS, ROWS), lambda r, p: (r // halo == q) & (p == first + r % halo)
                )
                start = j * wide + q * narrow
                packed = packed + place(picked, branch[:, start : start + narrow])
            back_out[side, j] = packed.astype(jnp.bfloat16)
            back_copy(side, j).start()

    own_back = one_hot((kmax, ROWS), lambda k, p: p == k + excess)
    live = lax.broadcasted_iota(jnp.int32, (kmax, narrow), 0) < here
    left_back, right_back = [], []
    for q in range(groups):
        left_back.append(one_hot(
            (kmax, ROWS), lambda k, r: (r == q * halo + halo + excess + k) & (k + excess < 0)
        ))
        right_back.append(one_hot(
            (kmax, ROWS),
            lambda k, r: (r == q * halo + excess + k - BAL)
            & (k + excess >= BAL) & (k + excess < BAL + halo),
        ))
    for j in range(groups):
        for side in range(2):
            back_copy(side, j).wait_recv()
        for q in range(groups):
            start = j * wide + q * narrow
            cols = slice(start, start + narrow)
            got = (
                place(own_back, branch[:, cols])
                + place(left_back[q], back_in[0, j])
                + place(right_back[q], back_in[1, j])
            )
            summed = g_ref[:, cols].astype(jnp.float32) + got
            out_ref[:, cols] = jnp.where(live, summed, 0.0).astype(jnp.bfloat16)

    for k in range(1, n_dp):
        count_copy(k, me).wait_send()
    for side in range(2):
        for i in range(2):
            halo_copy(side, i).wait_send()
        for j in range(groups):
            back_copy(side, j).wait_send()

    @pl.loop(0, steps)
    def _(step):
        for j in range(n_t):
            @pl.when((j <= t) & (t < n_t - 1))
            def _():
                in_copy(1, j, step).wait_send()

            @pl.when((j >= t) & (t > 0))
            def _():
                in_copy(0, j, step).wait_send()

    @pl.loop(0, chunks)
    def _(c):
        for k in range(1, n_t):
            term_copy(k, c, t).wait_send()


def fused(kept_input, kept_grad, up_weight_t, up_bias, down_weight, kept_count):
    n_dp, n_t = lax.axis_size("dp"), lax.axis_size("tensor")
    kmax, width = kept_input.shape
    hidden = up_weight_t.shape[0]
    chunks = width // COLS
    groups = ROWS // (BAL // 4)
    wide = width // groups
    narrow = wide // groups
    steps = 2 * groups
    tokens = n_t * ROWS
    bf16, f32 = jnp.bfloat16, jnp.float32
    vmem = pl.BlockSpec(memory_space=pltpu.VMEM)
    smem = pl.BlockSpec(memory_space=pltpu.SMEM)
    hbm = pl.BlockSpec(memory_space=pl.ANY)
    dma = pltpu.SemaphoreType.DMA
    return pl.pallas_call(
        functools.partial(fused_kernel, n_dp, n_t),
        out_shape=jax.ShapeDtypeStruct((kmax, width), bf16),
        in_specs=[vmem, vmem, smem, vmem, hbm, hbm],
        out_specs=vmem,
        scratch_shapes=[
            pltpu.VMEM((groups, hidden, wide), bf16),
            pltpu.VMEM((groups, hidden, wide), bf16),
            pltpu.VMEM((n_t, steps, ROWS, wide), bf16),
            pltpu.VMEM((chunks, n_t, ROWS, COLS), bf16),
            pltpu.VMEM((n_t, chunks, ROWS, COLS), bf16),
            pltpu.VMEM((ROWS, width), bf16),
            pltpu.VMEM((tokens, hidden), f32),
            pltpu.VMEM((tokens, hidden), f32),
            pltpu.VMEM((tokens, hidden), bf16),
            pltpu.VMEM((8, 128), jnp.int32),
            pltpu.VMEM((n_dp, 8, 128), jnp.int32),
            pltpu.VMEM((2, 2, ROWS, wide), bf16),
            pltpu.VMEM((2, 2, ROWS, wide), bf16),
            pltpu.VMEM((2, groups, ROWS, narrow), bf16),
            pltpu.VMEM((2, groups, ROWS, narrow), bf16),
            dma((2, groups)),
            dma((n_dp - 1,)),
            dma((n_dp,)),
            dma((2, 2)),
            dma((2, 2)),
            dma((2, groups)),
            dma((2, groups)),
            dma((2, n_t, steps)),
            dma((n_t, steps)),
            dma((n_t - 1, chunks)),
            dma((n_t, chunks)),
        ],
        compiler_params=pltpu.CompilerParams(
            collective_id=0, has_side_effects=True, vmem_limit_bytes=VMEM_LIMIT
        ),
    )(kept_input, kept_grad, kept_count, up_bias, up_weight_t, down_weight)


def fits(mesh, kept_input, up_weight_t):
    hidden = up_weight_t.shape[0] // mesh.shape["tensor"]
    width = up_weight_t.shape[1]
    weights = 2 * hidden * width * 2
    return (
        hidden % ROWS == 0
        and width % (COLS * 4) == 0
        and BAL == ROWS
        and mesh.shape["dp"] > 1
        and mesh.shape["tensor"] > 1
        and weights < VMEM_LIMIT * 3 // 4
    )


def solution(mesh):
    rows = P(("dp", "tensor"), None)
    placed = (rows, rows, P("tensor", None), P("tensor"), P("tensor", None), P(("dp", "tensor")))

    def run(kept_input, kept_grad, up_weight_t, up_bias, down_weight, kept_count):
        chosen = fused if fits(mesh, kept_input, up_weight_t) else body
        return jax.shard_map(
            chosen, mesh=mesh, in_specs=placed, out_specs=rows, check_vma=False
        )(kept_input, kept_grad, up_weight_t, up_bias, down_weight, kept_count)

    return run
```

```python
import functools

import jax
import jax.numpy as jnp
from jax import lax
from jax.experimental import pallas as pl
from jax.experimental.pallas import tpu as pltpu
from jax.sharding import PartitionSpec as P

BAL = 16


INV_SQRT_TWO = 0.7071067811865476
INV_SQRT_TWO_PI = 0.3989422804014327


def prefix(shard, axis, combine, identity):
    length, index = (lax.axis_size(axis), lax.axis_index(axis))
    everything = lax.all_gather(shard, axis)
    start = jnp.broadcast_to(jnp.asarray(identity, shard.dtype), shard.shape)

    def lap(k, before):
        reached = k < index
        new = combine(before, everything[k])
        return jnp.where(reached, new, before)

    return lax.fori_loop(0, length, lap, start)


def padded(block, sides, width):
    for axis, dim in sides:
        count = lax.axis_size(axis)
        forward = [(i, i + 1) for i in range(count - 1)]
        backward = [(target, source) for source, target in forward]
        low = lax.ppermute(
            lax.slice_in_dim(block, block.shape[dim] - width, None, axis=dim), axis, forward
        )
        high = lax.ppermute(lax.slice_in_dim(block, 0, width, axis=dim), axis, backward)
        block = jnp.concatenate([low, block, high], axis=dim)
    return block


def gelu_slope(values):
    return (
        0.5 * (1.0 + lax.erf(values * INV_SQRT_TWO))
        + values * jnp.exp(-0.5 * values * values) * INV_SQRT_TWO_PI
    )


def add_counts(earlier, later):
    return earlier + later


def ffn_rows(stacked, up_weight_t, up_bias, down_weight):
    contract = (((1,), (1,)), ((), ()))
    bias_wide = up_bias.astype(jnp.float32)
    piece_rows = lax.all_gather(stacked, "tensor", axis=0, tiled=True)
    inputs = piece_rows[:, 0]
    out_grads = piece_rows[:, 1]
    preact = (
        lax.dot_general(inputs, up_weight_t, contract, preferred_element_type=jnp.float32)
        + bias_wide
    )
    down_grad = lax.dot_general(
        out_grads, down_weight, contract, preferred_element_type=jnp.float32
    )
    pre_grad = (gelu_slope(preact) * down_grad).astype(jnp.bfloat16)
    partials = jnp.dot(pre_grad, up_weight_t, preferred_element_type=jnp.float32)
    return lax.psum_scatter(
        partials.astype(jnp.bfloat16), "tensor", scatter_dimension=0, tiled=True
    )


def body(kept_input, kept_grad, up_weight_t, up_bias, down_weight, kept_count):
    kmax = kept_input.shape[0]
    count_here = kept_count[0]
    entries = jnp.arange(kmax, dtype=jnp.int32)
    usable = entries < count_here
    stacked = jnp.stack((kept_input, kept_grad), axis=1)
    stacked = jnp.where(usable[:, None, None], stacked, jnp.zeros_like(stacked))
    halo_width = BAL // 4
    spots = BAL + 2 * halo_width
    first_slot = prefix(count_here, "dp", add_counts, jnp.int32(0))
    excess = first_slot - lax.axis_index("dp") * BAL
    target = excess + entries + halo_width
    placing = (target[None, :] == jnp.arange(spots, dtype=jnp.int32)[:, None]) & usable[None, :]
    placing_mat = placing.astype(jnp.bfloat16)
    outgoing = jnp.einsum(
        "sk,kcd->scd", placing_mat, stacked, preferred_element_type=jnp.float32
    ).astype(jnp.bfloat16)
    widened = padded(outgoing, (("dp", 0),), halo_width)
    owned = outgoing[halo_width : halo_width + BAL].astype(jnp.float32)
    owned = owned.at[:halo_width].add(widened[:halo_width].astype(jnp.float32))
    owned = owned.at[BAL - halo_width :].add(
        widened[widened.shape[0] - halo_width :].astype(jnp.float32)
    )
    branch = ffn_rows(owned.astype(jnp.bfloat16), up_weight_t, up_bias, down_weight)
    returned = padded(branch, (("dp", 0),), halo_width)
    own_branch = jnp.einsum(
        "sk,sd->kd", placing_mat, returned, preferred_element_type=jnp.float32
    ).astype(jnp.bfloat16)
    summed = kept_grad.astype(jnp.float32) + own_branch.astype(jnp.float32)
    return jnp.where(usable[:, None], summed, jnp.float32(0.0)).astype(jnp.bfloat16)


ROWS = 16
COLS = 512
VMEM_LIMIT = 58 * 1024 * 1024
MESH = pl.DeviceIdType.MESH
NT = (((1,), (1,)), ((), ()))


def one_hot(shape, picked):
    rows = lax.broadcasted_iota(jnp.int32, shape, 0)
    cols = lax.broadcasted_iota(jnp.int32, shape, 1)
    return picked(rows, cols).astype(jnp.float32).astype(jnp.bfloat16)


def place(matrix, block):
    return jnp.dot(matrix, block, preferred_element_type=jnp.float32)


def fused_kernel(
    n_dp, n_t, x_ref, g_ref, count_ref, bias_ref, up_hbm, down_hbm, out_ref,
    up, down, rows_in, terms, taken, branch, acc, slopes, pre_grad,
    count_own, counts, halo_out, halo_in, back_out, back_in,
    w_sem, count_send, count_recv, halo_send, halo_recv, back_send, back_recv,
    in_send, in_recv, term_send, term_recv,
):
    me = lax.axis_index("dp")
    t = lax.axis_index("tensor")
    kmax, width = x_ref.shape
    halo = BAL // 4
    groups = ROWS // halo
    wide = width // groups
    narrow = wide // groups
    per_group = wide // COLS
    chunks = width // COLS
    steps = 2 * groups
    left = lax.rem(me + n_dp - 1, n_dp)
    right = lax.rem(me + 1, n_dp)

    def weight_copy(i, j):
        source, target = ((up_hbm, up), (down_hbm, down))[i]
        cols = pl.ds(pl.multiple_of(j * wide, wide), wide)
        return pltpu.make_async_copy(source.at[:, cols], target.at[j], w_sem.at[i, j])

    for i in range(2):
        for j in range(groups):
            weight_copy(i, j).start()

    barrier = pltpu.get_barrier_semaphore()
    for k in range(1, n_dp):
        pl.semaphore_signal(
            barrier, inc=1, device_id={"dp": lax.rem(me + k, n_dp)}, device_id_type=MESH
        )
    for k in range(1, n_t):
        pl.semaphore_signal(
            barrier, inc=1, device_id={"tensor": lax.rem(t + k, n_t)}, device_id_type=MESH
        )

    here = count_ref[0]
    count_own[...] = jnp.full(count_own.shape, here, jnp.int32)
    for side in range(2):
        first = (here - halo) if side else 0
        for i, ref in enumerate((x_ref, g_ref)):
            packed = jnp.zeros((ROWS, wide), jnp.float32)
            for j in range(groups):
                picked = one_hot(
                    (ROWS, kmax), lambda r, k: (r // halo == j) & (k == first + r % halo)
                )
                packed = packed + place(picked, ref[:, j * wide : (j + 1) * wide])
            halo_out[side, i] = packed.astype(jnp.bfloat16)
    pl.semaphore_wait(barrier, n_dp - 1 + n_t - 1)

    def count_copy(k, source):
        return pltpu.make_async_remote_copy(
            src_ref=count_own, dst_ref=counts.at[source],
            send_sem=count_send.at[k - 1], recv_sem=count_recv.at[source],
            device_id={"dp": lax.rem(me + k, n_dp)}, device_id_type=MESH,
        )

    def halo_copy(side, i):
        return pltpu.make_async_remote_copy(
            src_ref=halo_out.at[side, i], dst_ref=halo_in.at[1 - side, i],
            send_sem=halo_send.at[side, i], recv_sem=halo_recv.at[1 - side, i],
            device_id={"dp": right if side else left}, device_id_type=MESH,
        )

    def back_copy(side, j):
        return pltpu.make_async_remote_copy(
            src_ref=back_out.at[side, j], dst_ref=back_in.at[1 - side, j],
            send_sem=back_send.at[side, j], recv_sem=back_recv.at[1 - side, j],
            device_id={"dp": right if side else left}, device_id_type=MESH,
        )

    for k in range(1, n_dp):
        count_copy(k, me).start()
    for i in range(2):
        for side in range(2):
            halo_copy(side, i).start()
    for k in range(1, n_dp):
        count_copy(k, lax.rem(me + n_dp - k, n_dp)).wait_recv()
    before = jnp.zeros(count_own.shape, jnp.int32)
    for j in range(n_dp):
        before = before + jnp.where(j < me, counts[j], 0)
    excess = (before - me * BAL)[0:1, 0:1]
    following = excess + here - BAL

    def in_copy(k, source, step):
        return pltpu.make_async_remote_copy(
            src_ref=rows_in.at[source, step], dst_ref=rows_in.at[source, step],
            send_sem=in_send.at[k - 1, step], recv_sem=in_recv.at[source, step],
            device_id={"tensor": lax.rem(t + k, n_t)}, device_id_type=MESH,
        )

    own_at = one_hot((ROWS, kmax), lambda p, k: (k == p - excess) & (k < here))
    from_left, from_right = [], []
    for j in range(groups):
        from_left.append(one_hot(
            (ROWS, ROWS), lambda p, r: (r == j * halo + halo - excess + p) & (p < excess)
        ))
        from_right.append(one_hot(
            (ROWS, ROWS),
            lambda p, r: (r == j * halo + p - BAL - following) & (p >= BAL + following),
        ))
    for i, ref in enumerate((x_ref, g_ref)):
        for side in range(2):
            halo_copy(side, i).wait_recv()
        for j in range(groups):
            rows_in[t, i * groups + j] = (
                place(own_at, ref[:, j * wide : (j + 1) * wide])
                + place(from_left[j], halo_in[0, i])
                + place(from_right[j], halo_in[1, i])
            ).astype(jnp.bfloat16)
            for k in range(1, n_t):
                in_copy(k, t, i * groups + j).start()

    def multiply(i, weights, first):
        acc[...] = first

        @pl.loop(0, groups)
        def _(j):
            step = i * groups + j
            for k in range(1, n_t):
                in_copy(k, lax.rem(t + n_t - k, n_t), step).wait_recv()
            weight_copy(i, j).wait()
            block = rows_in[:, step].reshape(n_t * ROWS, wide)
            acc[...] += lax.dot_general(
                block, weights[j], NT, preferred_element_type=jnp.float32
            )

    bias = bias_ref[...].astype(jnp.float32).reshape(1, acc.shape[1])
    multiply(0, up, jnp.broadcast_to(bias, acc.shape))
    slopes[...] = gelu_slope(acc[...])
    multiply(1, down, jnp.zeros(acc.shape, jnp.float32))
    pre_grad[...] = (slopes[...] * acc[...]).astype(jnp.bfloat16)

    def term_copy(k, c, source):
        dest = lax.rem(t + k, n_t)
        return pltpu.make_async_remote_copy(
            src_ref=terms.at[c, dest], dst_ref=taken.at[source, c],
            send_sem=term_send.at[k - 1, c], recv_sem=term_recv.at[source, c],
            device_id={"tensor": dest}, device_id_type=MESH,
        )

    @pl.loop(0, groups)
    def _(j):
        for s in range(per_group):
            c = j * per_group + s
            term = jnp.dot(
                pre_grad[...], up[j, :, s * COLS : (s + 1) * COLS],
                preferred_element_type=jnp.float32,
            )
            terms[c] = term.astype(jnp.bfloat16).reshape(n_t, ROWS, COLS)
            for k in range(1, n_t):
                term_copy(k, c, t).start()

    for j in range(groups):
        for s in range(per_group):
            c = j * per_group + s
            total = terms[c, t].astype(jnp.float32)
            for k in range(1, n_t):
                source = lax.rem(t + n_t - k, n_t)
                term_copy(k, c, source).wait_recv()
                total = total + taken[source, c].astype(jnp.float32)
            branch[:, c * COLS : (c + 1) * COLS] = total.astype(jnp.bfloat16)
        for side in range(2):
            first = (BAL - halo) if side else 0
            packed = jnp.zeros((ROWS, narrow), jnp.float32)
            for q in range(groups):
                picked = one_hot(
                    (ROWS, ROWS), lambda r, p: (r // halo == q) & (p == first + r % halo)
                )
                start = j * wide + q * narrow
                packed = packed + place(picked, branch[:, start : start + narrow])
            back_out[side, j] = packed.astype(jnp.bfloat16)
            back_copy(side, j).start()

    own_back = one_hot((kmax, ROWS), lambda k, p: p == k + excess)
    live = lax.broadcasted_iota(jnp.int32, (kmax, narrow), 0) < here
    left_back, right_back = [], []
    for q in range(groups):
        left_back.append(one_hot(
            (kmax, ROWS), lambda k, r: (r == q * halo + halo + excess + k) & (k + excess < 0)
        ))
        right_back.append(one_hot(
            (kmax, ROWS),
            lambda k, r: (r == q * halo + excess + k - BAL)
            & (k + excess >= BAL) & (k + excess < BAL + halo),
        ))
    for j in range(groups):
        for side in range(2):
            back_copy(side, j).wait_recv()
        for q in range(groups):
            start = j * wide + q * narrow
            cols = slice(start, start + narrow)
            got = (
                place(own_back, branch[:, cols])
                + place(left_back[q], back_in[0, j])
                + place(right_back[q], back_in[1, j])
            )
            summed = g_ref[:, cols].astype(jnp.float32) + got
            out_ref[:, cols] = jnp.where(live, summed, 0.0).astype(jnp.bfloat16)

    for k in range(1, n_dp):
        count_copy(k, me).wait_send()
    for side in range(2):
        for i in range(2):
            halo_copy(side, i).wait_send()
        for j in range(groups):
            back_copy(side, j).wait_send()

    @pl.loop(0, steps)
    def _(step):
        for k in range(1, n_t):
            in_copy(k, t, step).wait_send()

    @pl.loop(0, chunks)
    def _(c):
        for k in range(1, n_t):
            term_copy(k, c, t).wait_send()


def fused(kept_input, kept_grad, up_weight_t, up_bias, down_weight, kept_count):
    n_dp, n_t = lax.axis_size("dp"), lax.axis_size("tensor")
    kmax, width = kept_input.shape
    hidden = up_weight_t.shape[0]
    chunks = width // COLS
    groups = ROWS // (BAL // 4)
    wide = width // groups
    narrow = wide // groups
    steps = 2 * groups
    tokens = n_t * ROWS
    bf16, f32 = jnp.bfloat16, jnp.float32
    vmem = pl.BlockSpec(memory_space=pltpu.VMEM)
    smem = pl.BlockSpec(memory_space=pltpu.SMEM)
    hbm = pl.BlockSpec(memory_space=pl.ANY)
    dma = pltpu.SemaphoreType.DMA
    return pl.pallas_call(
        functools.partial(fused_kernel, n_dp, n_t),
        out_shape=jax.ShapeDtypeStruct((kmax, width), bf16),
        in_specs=[vmem, vmem, smem, vmem, hbm, hbm],
        out_specs=vmem,
        scratch_shapes=[
            pltpu.VMEM((groups, hidden, wide), bf16),
            pltpu.VMEM((groups, hidden, wide), bf16),
            pltpu.VMEM((n_t, steps, ROWS, wide), bf16),
            pltpu.VMEM((chunks, n_t, ROWS, COLS), bf16),
            pltpu.VMEM((n_t, chunks, ROWS, COLS), bf16),
            pltpu.VMEM((ROWS, width), bf16),
            pltpu.VMEM((tokens, hidden), f32),
            pltpu.VMEM((tokens, hidden), f32),
            pltpu.VMEM((tokens, hidden), bf16),
            pltpu.VMEM((8, 128), jnp.int32),
            pltpu.VMEM((n_dp, 8, 128), jnp.int32),
            pltpu.VMEM((2, 2, ROWS, wide), bf16),
            pltpu.VMEM((2, 2, ROWS, wide), bf16),
            pltpu.VMEM((2, groups, ROWS, narrow), bf16),
            pltpu.VMEM((2, groups, ROWS, narrow), bf16),
            dma((2, groups)),
            dma((n_dp - 1,)),
            dma((n_dp,)),
            dma((2, 2)),
            dma((2, 2)),
            dma((2, groups)),
            dma((2, groups)),
            dma((n_t - 1, steps)),
            dma((n_t, steps)),
            dma((n_t - 1, chunks)),
            dma((n_t, chunks)),
        ],
        compiler_params=pltpu.CompilerParams(
            collective_id=0, has_side_effects=True, vmem_limit_bytes=VMEM_LIMIT
        ),
    )(kept_input, kept_grad, kept_count, up_bias, up_weight_t, down_weight)


def fits(mesh, kept_input, up_weight_t):
    hidden = up_weight_t.shape[0] // mesh.shape["tensor"]
    width = up_weight_t.shape[1]
    weights = 2 * hidden * width * 2
    return (
        hidden % ROWS == 0
        and width % (COLS * 4) == 0
        and BAL == ROWS
        and mesh.shape["dp"] > 1
        and mesh.shape["tensor"] > 1
        and weights < VMEM_LIMIT * 3 // 4
    )


def solution(mesh):
    rows = P(("dp", "tensor"), None)
    placed = (rows, rows, P("tensor", None), P("tensor"), P("tensor", None), P(("dp", "tensor")))

    def run(kept_input, kept_grad, up_weight_t, up_bias, down_weight, kept_count):
        chosen = fused if fits(mesh, kept_input, up_weight_t) else body
        return jax.shard_map(
            chosen, mesh=mesh, in_specs=placed, out_specs=rows, check_vma=False
        )(kept_input, kept_grad, up_weight_t, up_bias, down_weight, kept_count)

    return run
```

```python
import functools

import jax
import jax.numpy as jnp
from jax import lax
from jax.experimental import pallas as pl
from jax.experimental.pallas import tpu as pltpu
from jax.sharding import PartitionSpec as P

BAL = 16


INV_SQRT_TWO = 0.7071067811865476
INV_SQRT_TWO_PI = 0.3989422804014327


def prefix(shard, axis, combine, identity):
    length, index = (lax.axis_size(axis), lax.axis_index(axis))
    everything = lax.all_gather(shard, axis)
    start = jnp.broadcast_to(jnp.asarray(identity, shard.dtype), shard.shape)

    def lap(k, before):
        reached = k < index
        new = combine(before, everything[k])
        return jnp.where(reached, new, before)

    return lax.fori_loop(0, length, lap, start)


def padded(block, sides, width):
    for axis, dim in sides:
        count = lax.axis_size(axis)
        forward = [(i, i + 1) for i in range(count - 1)]
        backward = [(target, source) for source, target in forward]
        low = lax.ppermute(
            lax.slice_in_dim(block, block.shape[dim] - width, None, axis=dim), axis, forward
        )
        high = lax.ppermute(lax.slice_in_dim(block, 0, width, axis=dim), axis, backward)
        block = jnp.concatenate([low, block, high], axis=dim)
    return block


def gelu_slope(values):
    return (
        0.5 * (1.0 + lax.erf(values * INV_SQRT_TWO))
        + values * jnp.exp(-0.5 * values * values) * INV_SQRT_TWO_PI
    )


def add_counts(earlier, later):
    return earlier + later


def ffn_rows(stacked, up_weight_t, up_bias, down_weight):
    contract = (((1,), (1,)), ((), ()))
    bias_wide = up_bias.astype(jnp.float32)
    piece_rows = lax.all_gather(stacked, "tensor", axis=0, tiled=True)
    inputs = piece_rows[:, 0]
    out_grads = piece_rows[:, 1]
    preact = (
        lax.dot_general(inputs, up_weight_t, contract, preferred_element_type=jnp.float32)
        + bias_wide
    )
    down_grad = lax.dot_general(
        out_grads, down_weight, contract, preferred_element_type=jnp.float32
    )
    pre_grad = (gelu_slope(preact) * down_grad).astype(jnp.bfloat16)
    partials = jnp.dot(pre_grad, up_weight_t, preferred_element_type=jnp.float32)
    return lax.psum_scatter(
        partials.astype(jnp.bfloat16), "tensor", scatter_dimension=0, tiled=True
    )


def body(kept_input, kept_grad, up_weight_t, up_bias, down_weight, kept_count):
    kmax = kept_input.shape[0]
    count_here = kept_count[0]
    entries = jnp.arange(kmax, dtype=jnp.int32)
    usable = entries < count_here
    stacked = jnp.stack((kept_input, kept_grad), axis=1)
    stacked = jnp.where(usable[:, None, None], stacked, jnp.zeros_like(stacked))
    halo_width = BAL // 4
    spots = BAL + 2 * halo_width
    first_slot = prefix(count_here, "dp", add_counts, jnp.int32(0))
    excess = first_slot - lax.axis_index("dp") * BAL
    target = excess + entries + halo_width
    placing = (target[None, :] == jnp.arange(spots, dtype=jnp.int32)[:, None]) & usable[None, :]
    placing_mat = placing.astype(jnp.bfloat16)
    outgoing = jnp.einsum(
        "sk,kcd->scd", placing_mat, stacked, preferred_element_type=jnp.float32
    ).astype(jnp.bfloat16)
    widened = padded(outgoing, (("dp", 0),), halo_width)
    owned = outgoing[halo_width : halo_width + BAL].astype(jnp.float32)
    owned = owned.at[:halo_width].add(widened[:halo_width].astype(jnp.float32))
    owned = owned.at[BAL - halo_width :].add(
        widened[widened.shape[0] - halo_width :].astype(jnp.float32)
    )
    branch = ffn_rows(owned.astype(jnp.bfloat16), up_weight_t, up_bias, down_weight)
    returned = padded(branch, (("dp", 0),), halo_width)
    own_branch = jnp.einsum(
        "sk,sd->kd", placing_mat, returned, preferred_element_type=jnp.float32
    ).astype(jnp.bfloat16)
    summed = kept_grad.astype(jnp.float32) + own_branch.astype(jnp.float32)
    return jnp.where(usable[:, None], summed, jnp.float32(0.0)).astype(jnp.bfloat16)


ROWS = 16
COLS = 512
VMEM_LIMIT = 58 * 1024 * 1024
MESH = pl.DeviceIdType.MESH
NT = (((1,), (1,)), ((), ()))


def one_hot(shape, picked):
    rows = lax.broadcasted_iota(jnp.int32, shape, 0)
    cols = lax.broadcasted_iota(jnp.int32, shape, 1)
    return picked(rows, cols).astype(jnp.float32).astype(jnp.bfloat16)


def place(matrix, block):
    return jnp.dot(matrix, block, preferred_element_type=jnp.float32)


def fused_kernel(
    n_dp, n_t, x_ref, g_ref, count_ref, bias_ref, up_hbm, down_hbm, out_ref,
    up, down, rows_in, terms, taken, branch, acc, slopes, pre_grad,
    count_own, counts, halo_out, halo_in, back_out, back_in,
    w_sem, count_send, count_recv, halo_send, halo_recv, back_send, back_recv,
    in_send, in_recv, term_send, term_recv,
):
    me = lax.axis_index("dp")
    t = lax.axis_index("tensor")
    kmax, width = x_ref.shape
    halo = BAL // 4
    groups = ROWS // halo
    wide = width // groups
    narrow = wide // groups
    per_group = wide // COLS
    chunks = width // COLS
    steps = 2 * groups
    left = lax.rem(me + n_dp - 1, n_dp)
    right = lax.rem(me + 1, n_dp)

    def weight_copy(i, j):
        source, target = ((up_hbm, up), (down_hbm, down))[i]
        cols = pl.ds(pl.multiple_of(j * wide, wide), wide)
        return pltpu.make_async_copy(source.at[:, cols], target.at[j], w_sem.at[i, j])

    for i in range(2):
        for j in range(groups):
            weight_copy(i, j).start()

    barrier = pltpu.get_barrier_semaphore()
    for k in range(1, n_dp):
        pl.semaphore_signal(
            barrier, inc=1, device_id={"dp": lax.rem(me + k, n_dp)}, device_id_type=MESH
        )
    for k in range(1, n_t):
        pl.semaphore_signal(
            barrier, inc=1, device_id={"tensor": lax.rem(t + k, n_t)}, device_id_type=MESH
        )

    here = count_ref[0]
    count_own[...] = jnp.full(count_own.shape, here, jnp.int32)
    for side in range(2):
        first = (here - halo) if side else 0
        for i, ref in enumerate((x_ref, g_ref)):
            packed = jnp.zeros((ROWS, wide), jnp.float32)
            for j in range(groups):
                picked = one_hot(
                    (ROWS, kmax), lambda r, k: (r // halo == j) & (k == first + r % halo)
                )
                packed = packed + place(picked, ref[:, j * wide : (j + 1) * wide])
            halo_out[side, i] = packed.astype(jnp.bfloat16)
    pl.semaphore_wait(barrier, n_dp - 1 + n_t - 1)

    def count_copy(k, source):
        return pltpu.make_async_remote_copy(
            src_ref=count_own, dst_ref=counts.at[source],
            send_sem=count_send.at[k - 1], recv_sem=count_recv.at[source],
            device_id={"dp": lax.rem(me + k, n_dp)}, device_id_type=MESH,
        )

    def halo_copy(side, i):
        return pltpu.make_async_remote_copy(
            src_ref=halo_out.at[side, i], dst_ref=halo_in.at[1 - side, i],
            send_sem=halo_send.at[side, i], recv_sem=halo_recv.at[1 - side, i],
            device_id={"dp": right if side else left}, device_id_type=MESH,
        )

    def back_copy(side, j):
        return pltpu.make_async_remote_copy(
            src_ref=back_out.at[side, j], dst_ref=back_in.at[1 - side, j],
            send_sem=back_send.at[side, j], recv_sem=back_recv.at[1 - side, j],
            device_id={"dp": right if side else left}, device_id_type=MESH,
        )

    for k in range(1, n_dp):
        count_copy(k, me).start()
    for i in range(2):
        for side in range(2):
            halo_copy(side, i).start()
    for k in range(1, n_dp):
        count_copy(k, lax.rem(me + n_dp - k, n_dp)).wait_recv()
    before = jnp.zeros(count_own.shape, jnp.int32)
    for j in range(n_dp):
        before = before + jnp.where(j < me, counts[j], 0)
    excess = (before - me * BAL)[0:1, 0:1]
    following = excess + here - BAL

    def in_copy(k, source, step):
        return pltpu.make_async_remote_copy(
            src_ref=rows_in.at[source, step], dst_ref=rows_in.at[source, step],
            send_sem=in_send.at[k - 1, step], recv_sem=in_recv.at[source, step],
            device_id={"tensor": lax.rem(t + k, n_t)}, device_id_type=MESH,
        )

    own_at = one_hot((ROWS, kmax), lambda p, k: (k == p - excess) & (k < here))
    from_left, from_right = [], []
    for j in range(groups):
        from_left.append(one_hot(
            (ROWS, ROWS), lambda p, r: (r == j * halo + halo - excess + p) & (p < excess)
        ))
        from_right.append(one_hot(
            (ROWS, ROWS),
            lambda p, r: (r == j * halo + p - BAL - following) & (p >= BAL + following),
        ))
    for i, ref in enumerate((x_ref, g_ref)):
        for side in range(2):
            halo_copy(side, i).wait_recv()
        for j in range(groups):
            rows_in[t, i * groups + j] = (
                place(own_at, ref[:, j * wide : (j + 1) * wide])
                + place(from_left[j], halo_in[0, i])
                + place(from_right[j], halo_in[1, i])
            ).astype(jnp.bfloat16)
            for k in range(1, n_t):
                in_copy(k, t, i * groups + j).start()

    def multiply(i, weights):
        acc[...] = jnp.zeros_like(acc)

        @pl.loop(0, groups)
        def _(j):
            step = i * groups + j
            for k in range(1, n_t):
                in_copy(k, lax.rem(t + n_t - k, n_t), step).wait_recv()
            weight_copy(i, j).wait()
            block = rows_in[:, step].reshape(n_t * ROWS, wide)
            acc[...] += lax.dot_general(
                weights[j], block, NT, preferred_element_type=jnp.float32
            )

    bias = bias_ref[...].astype(jnp.float32).reshape(1, slopes.shape[1])
    multiply(0, up)
    slopes[...] = gelu_slope(acc[...].T + bias)
    multiply(1, down)
    pre_grad[...] = (slopes[...] * acc[...].T).astype(jnp.bfloat16)

    def term_copy(k, c, source):
        dest = lax.rem(t + k, n_t)
        return pltpu.make_async_remote_copy(
            src_ref=terms.at[c, dest], dst_ref=taken.at[source, c],
            send_sem=term_send.at[k - 1, c], recv_sem=term_recv.at[source, c],
            device_id={"tensor": dest}, device_id_type=MESH,
        )

    @pl.loop(0, groups)
    def _(j):
        for s in range(per_group):
            c = j * per_group + s
            term = jnp.dot(
                pre_grad[...], up[j, :, s * COLS : (s + 1) * COLS],
                preferred_element_type=jnp.float32,
            )
            terms[c] = term.astype(jnp.bfloat16).reshape(n_t, ROWS, COLS)
            for k in range(1, n_t):
                term_copy(k, c, t).start()

    for j in range(groups):
        for s in range(per_group):
            c = j * per_group + s
            total = terms[c, t].astype(jnp.float32)
            for k in range(1, n_t):
                source = lax.rem(t + n_t - k, n_t)
                term_copy(k, c, source).wait_recv()
                total = total + taken[source, c].astype(jnp.float32)
            branch[:, c * COLS : (c + 1) * COLS] = total.astype(jnp.bfloat16)
        for side in range(2):
            first = (BAL - halo) if side else 0
            packed = jnp.zeros((ROWS, narrow), jnp.float32)
            for q in range(groups):
                picked = one_hot(
                    (ROWS, ROWS), lambda r, p: (r // halo == q) & (p == first + r % halo)
                )
                start = j * wide + q * narrow
                packed = packed + place(picked, branch[:, start : start + narrow])
            back_out[side, j] = packed.astype(jnp.bfloat16)
            back_copy(side, j).start()

    own_back = one_hot((kmax, ROWS), lambda k, p: p == k + excess)
    live = lax.broadcasted_iota(jnp.int32, (kmax, narrow), 0) < here
    left_back, right_back = [], []
    for q in range(groups):
        left_back.append(one_hot(
            (kmax, ROWS), lambda k, r: (r == q * halo + halo + excess + k) & (k + excess < 0)
        ))
        right_back.append(one_hot(
            (kmax, ROWS),
            lambda k, r: (r == q * halo + excess + k - BAL)
            & (k + excess >= BAL) & (k + excess < BAL + halo),
        ))
    for j in range(groups):
        for side in range(2):
            back_copy(side, j).wait_recv()
        for q in range(groups):
            start = j * wide + q * narrow
            cols = slice(start, start + narrow)
            got = (
                place(own_back, branch[:, cols])
                + place(left_back[q], back_in[0, j])
                + place(right_back[q], back_in[1, j])
            )
            summed = g_ref[:, cols].astype(jnp.float32) + got
            out_ref[:, cols] = jnp.where(live, summed, 0.0).astype(jnp.bfloat16)

    for k in range(1, n_dp):
        count_copy(k, me).wait_send()
    for side in range(2):
        for i in range(2):
            halo_copy(side, i).wait_send()
        for j in range(groups):
            back_copy(side, j).wait_send()

    @pl.loop(0, steps)
    def _(step):
        for k in range(1, n_t):
            in_copy(k, t, step).wait_send()

    @pl.loop(0, chunks)
    def _(c):
        for k in range(1, n_t):
            term_copy(k, c, t).wait_send()


def fused(kept_input, kept_grad, up_weight_t, up_bias, down_weight, kept_count):
    n_dp, n_t = lax.axis_size("dp"), lax.axis_size("tensor")
    kmax, width = kept_input.shape
    hidden = up_weight_t.shape[0]
    chunks = width // COLS
    groups = ROWS // (BAL // 4)
    wide = width // groups
    narrow = wide // groups
    steps = 2 * groups
    tokens = n_t * ROWS
    bf16, f32 = jnp.bfloat16, jnp.float32
    vmem = pl.BlockSpec(memory_space=pltpu.VMEM)
    smem = pl.BlockSpec(memory_space=pltpu.SMEM)
    hbm = pl.BlockSpec(memory_space=pl.ANY)
    dma = pltpu.SemaphoreType.DMA
    return pl.pallas_call(
        functools.partial(fused_kernel, n_dp, n_t),
        out_shape=jax.ShapeDtypeStruct((kmax, width), bf16),
        in_specs=[vmem, vmem, smem, vmem, hbm, hbm],
        out_specs=vmem,
        scratch_shapes=[
            pltpu.VMEM((groups, hidden, wide), bf16),
            pltpu.VMEM((groups, hidden, wide), bf16),
            pltpu.VMEM((n_t, steps, ROWS, wide), bf16),
            pltpu.VMEM((chunks, n_t, ROWS, COLS), bf16),
            pltpu.VMEM((n_t, chunks, ROWS, COLS), bf16),
            pltpu.VMEM((ROWS, width), bf16),
            pltpu.VMEM((hidden, tokens), f32),
            pltpu.VMEM((tokens, hidden), f32),
            pltpu.VMEM((tokens, hidden), bf16),
            pltpu.VMEM((8, 128), jnp.int32),
            pltpu.VMEM((n_dp, 8, 128), jnp.int32),
            pltpu.VMEM((2, 2, ROWS, wide), bf16),
            pltpu.VMEM((2, 2, ROWS, wide), bf16),
            pltpu.VMEM((2, groups, ROWS, narrow), bf16),
            pltpu.VMEM((2, groups, ROWS, narrow), bf16),
            dma((2, groups)),
            dma((n_dp - 1,)),
            dma((n_dp,)),
            dma((2, 2)),
            dma((2, 2)),
            dma((2, groups)),
            dma((2, groups)),
            dma((n_t - 1, steps)),
            dma((n_t, steps)),
            dma((n_t - 1, chunks)),
            dma((n_t, chunks)),
        ],
        compiler_params=pltpu.CompilerParams(
            collective_id=0, has_side_effects=True, vmem_limit_bytes=VMEM_LIMIT
        ),
    )(kept_input, kept_grad, kept_count, up_bias, up_weight_t, down_weight)


def fits(mesh, kept_input, up_weight_t):
    hidden = up_weight_t.shape[0] // mesh.shape["tensor"]
    width = up_weight_t.shape[1]
    weights = 2 * hidden * width * 2
    return (
        hidden % ROWS == 0
        and width % (COLS * 4) == 0
        and BAL == ROWS
        and mesh.shape["dp"] > 1
        and mesh.shape["tensor"] > 1
        and weights < VMEM_LIMIT * 3 // 4
    )


def solution(mesh):
    rows = P(("dp", "tensor"), None)
    placed = (rows, rows, P("tensor", None), P("tensor"), P("tensor", None), P(("dp", "tensor")))

    def run(kept_input, kept_grad, up_weight_t, up_bias, down_weight, kept_count):
        chosen = fused if fits(mesh, kept_input, up_weight_t) else body
        return jax.shard_map(
            chosen, mesh=mesh, in_specs=placed, out_specs=rows, check_vma=False
        )(kept_input, kept_grad, up_weight_t, up_bias, down_weight, kept_count)

    return run
```

```python
import functools

import jax
import jax.numpy as jnp
from jax import lax
from jax.experimental import pallas as pl
from jax.experimental.pallas import tpu as pltpu
from jax.sharding import PartitionSpec as P

BAL = 16


INV_SQRT_TWO = 0.7071067811865476
INV_SQRT_TWO_PI = 0.3989422804014327


def prefix(shard, axis, combine, identity):
    length, index = (lax.axis_size(axis), lax.axis_index(axis))
    everything = lax.all_gather(shard, axis)
    start = jnp.broadcast_to(jnp.asarray(identity, shard.dtype), shard.shape)

    def lap(k, before):
        reached = k < index
        new = combine(before, everything[k])
        return jnp.where(reached, new, before)

    return lax.fori_loop(0, length, lap, start)


def padded(block, sides, width):
    for axis, dim in sides:
        count = lax.axis_size(axis)
        forward = [(i, i + 1) for i in range(count - 1)]
        backward = [(target, source) for source, target in forward]
        low = lax.ppermute(
            lax.slice_in_dim(block, block.shape[dim] - width, None, axis=dim), axis, forward
        )
        high = lax.ppermute(lax.slice_in_dim(block, 0, width, axis=dim), axis, backward)
        block = jnp.concatenate([low, block, high], axis=dim)
    return block


def gelu_slope(values):
    return (
        0.5 * (1.0 + lax.erf(values * INV_SQRT_TWO))
        + values * jnp.exp(-0.5 * values * values) * INV_SQRT_TWO_PI
    )


def add_counts(earlier, later):
    return earlier + later


def ffn_rows(stacked, up_weight_t, up_bias, down_weight):
    contract = (((1,), (1,)), ((), ()))
    bias_wide = up_bias.astype(jnp.float32)
    piece_rows = lax.all_gather(stacked, "tensor", axis=0, tiled=True)
    inputs = piece_rows[:, 0]
    out_grads = piece_rows[:, 1]
    preact = (
        lax.dot_general(inputs, up_weight_t, contract, preferred_element_type=jnp.float32)
        + bias_wide
    )
    down_grad = lax.dot_general(
        out_grads, down_weight, contract, preferred_element_type=jnp.float32
    )
    pre_grad = (gelu_slope(preact) * down_grad).astype(jnp.bfloat16)
    partials = jnp.dot(pre_grad, up_weight_t, preferred_element_type=jnp.float32)
    return lax.psum_scatter(
        partials.astype(jnp.bfloat16), "tensor", scatter_dimension=0, tiled=True
    )


def body(kept_input, kept_grad, up_weight_t, up_bias, down_weight, kept_count):
    kmax = kept_input.shape[0]
    count_here = kept_count[0]
    entries = jnp.arange(kmax, dtype=jnp.int32)
    usable = entries < count_here
    stacked = jnp.stack((kept_input, kept_grad), axis=1)
    stacked = jnp.where(usable[:, None, None], stacked, jnp.zeros_like(stacked))
    halo_width = BAL // 4
    spots = BAL + 2 * halo_width
    first_slot = prefix(count_here, "dp", add_counts, jnp.int32(0))
    excess = first_slot - lax.axis_index("dp") * BAL
    target = excess + entries + halo_width
    placing = (target[None, :] == jnp.arange(spots, dtype=jnp.int32)[:, None]) & usable[None, :]
    placing_mat = placing.astype(jnp.bfloat16)
    outgoing = jnp.einsum(
        "sk,kcd->scd", placing_mat, stacked, preferred_element_type=jnp.float32
    ).astype(jnp.bfloat16)
    widened = padded(outgoing, (("dp", 0),), halo_width)
    owned = outgoing[halo_width : halo_width + BAL].astype(jnp.float32)
    owned = owned.at[:halo_width].add(widened[:halo_width].astype(jnp.float32))
    owned = owned.at[BAL - halo_width :].add(
        widened[widened.shape[0] - halo_width :].astype(jnp.float32)
    )
    branch = ffn_rows(owned.astype(jnp.bfloat16), up_weight_t, up_bias, down_weight)
    returned = padded(branch, (("dp", 0),), halo_width)
    own_branch = jnp.einsum(
        "sk,sd->kd", placing_mat, returned, preferred_element_type=jnp.float32
    ).astype(jnp.bfloat16)
    summed = kept_grad.astype(jnp.float32) + own_branch.astype(jnp.float32)
    return jnp.where(usable[:, None], summed, jnp.float32(0.0)).astype(jnp.bfloat16)


ROWS = 16
COLS = 512
LEAD = 3
VMEM_LIMIT = 58 * 1024 * 1024
MESH = pl.DeviceIdType.MESH
NT = (((1,), (1,)), ((), ()))


def one_hot(shape, picked):
    rows = lax.broadcasted_iota(jnp.int32, shape, 0)
    cols = lax.broadcasted_iota(jnp.int32, shape, 1)
    return picked(rows, cols).astype(jnp.float32).astype(jnp.bfloat16)


def place(matrix, block):
    return jnp.dot(matrix, block, preferred_element_type=jnp.float32)


def fused_kernel(
    n_dp, n_t, x_ref, g_ref, count_ref, bias_ref, up_hbm, down_hbm, out_ref,
    up, down, rows_in, terms, taken, branch, acc, slopes, pre_grad,
    count_own, counts, halo_out, halo_in, back_out, back_in,
    w_sem, count_send, count_recv, halo_send, halo_recv, back_send, back_recv,
    in_send, in_recv, relay_send, term_send, term_recv,
):
    me = lax.axis_index("dp")
    t = lax.axis_index("tensor")
    kmax, width = x_ref.shape
    halo = BAL // 4
    groups = ROWS // halo
    wide = width // groups
    narrow = wide // groups
    per_group = wide // COLS
    chunks = width // COLS
    steps = 2 * groups
    left = lax.rem(me + n_dp - 1, n_dp)
    right = lax.rem(me + 1, n_dp)

    def weight_copy(i, j):
        source, target = ((up_hbm, up), (down_hbm, down))[i]
        cols = pl.ds(pl.multiple_of(j * wide, wide), wide)
        return pltpu.make_async_copy(source.at[:, cols], target.at[j], w_sem.at[i, j])

    for i in range(2):
        for j in range(groups):
            weight_copy(i, j).start()

    barrier = pltpu.get_barrier_semaphore()
    for k in range(1, n_dp):
        pl.semaphore_signal(
            barrier, inc=1, device_id={"dp": lax.rem(me + k, n_dp)}, device_id_type=MESH
        )
    for k in range(1, n_t):
        pl.semaphore_signal(
            barrier, inc=1, device_id={"tensor": lax.rem(t + k, n_t)}, device_id_type=MESH
        )

    here = count_ref[0]
    count_own[...] = jnp.full(count_own.shape, here, jnp.int32)
    for side in range(2):
        first = (here - halo) if side else 0
        for i, ref in enumerate((x_ref, g_ref)):
            packed = jnp.zeros((ROWS, wide), jnp.float32)
            for j in range(groups):
                picked = one_hot(
                    (ROWS, kmax), lambda r, k: (r // halo == j) & (k == first + r % halo)
                )
                packed = packed + place(picked, ref[:, j * wide : (j + 1) * wide])
            halo_out[side, i] = packed.astype(jnp.bfloat16)
    pl.semaphore_wait(barrier, n_dp - 1 + n_t - 1)

    def count_copy(k, source):
        return pltpu.make_async_remote_copy(
            src_ref=count_own, dst_ref=counts.at[source],
            send_sem=count_send.at[k - 1], recv_sem=count_recv.at[source],
            device_id={"dp": lax.rem(me + k, n_dp)}, device_id_type=MESH,
        )

    def halo_copy(side, i):
        return pltpu.make_async_remote_copy(
            src_ref=halo_out.at[side, i], dst_ref=halo_in.at[1 - side, i],
            send_sem=halo_send.at[side, i], recv_sem=halo_recv.at[1 - side, i],
            device_id={"dp": right if side else left}, device_id_type=MESH,
        )

    def back_copy(side, j):
        return pltpu.make_async_remote_copy(
            src_ref=back_out.at[side, j], dst_ref=back_in.at[1 - side, j],
            send_sem=back_send.at[side, j], recv_sem=back_recv.at[1 - side, j],
            device_id={"dp": right if side else left}, device_id_type=MESH,
        )

    for k in range(1, n_dp):
        count_copy(k, me).start()
    for i in range(2):
        for side in range(2):
            halo_copy(side, i).start()
    for k in range(1, n_dp):
        count_copy(k, lax.rem(me + n_dp - k, n_dp)).wait_recv()
    before = jnp.zeros(count_own.shape, jnp.int32)
    for j in range(n_dp):
        before = before + jnp.where(j < me, counts[j], 0)
    excess = (before - me * BAL)[0:1, 0:1]
    following = excess + here - BAL

    def in_copy(k, source, step):
        return pltpu.make_async_remote_copy(
            src_ref=rows_in.at[source, step], dst_ref=rows_in.at[source, step],
            send_sem=in_send.at[k - 1, step], recv_sem=in_recv.at[source, step],
            device_id={"tensor": lax.rem(t + k, n_t)}, device_id_type=MESH,
        )

    def relay_copy(source, step):
        return pltpu.make_async_remote_copy(
            src_ref=rows_in.at[source, step], dst_ref=rows_in.at[source, step],
            send_sem=relay_send.at[0 if source else 1, step],
            recv_sem=in_recv.at[source, step],
            device_id={"tensor": n_t - 1 - source}, device_id_type=MESH,
        )

    relays = (0, n_t - 1) if n_t > 2 else ()

    def relay_at(source):
        return t == (1 if source else n_t - 2)

    def sends(k):
        dest = lax.rem(t + k, n_t)
        return jnp.abs(dest - t) < n_t - (1 if relays else 0)

    def start_own(step):
        for k in range(1, n_t):
            @pl.when(sends(k))
            def _():
                in_copy(k, t, step).start()

    own_at = one_hot((ROWS, kmax), lambda p, k: (k == p - excess) & (k < here))
    from_left, from_right = [], []
    for j in range(groups):
        from_left.append(one_hot(
            (ROWS, ROWS), lambda p, r: (r == j * halo + halo - excess + p) & (p < excess)
        ))
        from_right.append(one_hot(
            (ROWS, ROWS),
            lambda p, r: (r == j * halo + p - BAL - following) & (p >= BAL + following),
        ))
    for i, ref in enumerate((x_ref, g_ref)):
        for side in range(2):
            halo_copy(side, i).wait_recv()
        for j in range(groups):
            rows_in[t, i * groups + j] = (
                place(own_at, ref[:, j * wide : (j + 1) * wide])
                + place(from_left[j], halo_in[0, i])
                + place(from_right[j], halo_in[1, i])
            ).astype(jnp.bfloat16)
            if i * groups + j < LEAD:
                start_own(i * groups + j)

    def multiply(i, weights, first):
        acc[...] = first

        @pl.loop(0, groups)
        def _(j):
            step = i * groups + j
            for source in relays:
                @pl.when(relay_at(source))
                def _():
                    in_copy(1, source, step).wait_recv()
                    relay_copy(source, step).start()

            @pl.when(step + LEAD < steps)
            def _():
                start_own(step + LEAD)

            for k in range(1, n_t):
                source = lax.rem(t + n_t - k, n_t)
                waiting = k > 0
                for end in relays:
                    waiting = waiting & ((source != end) | jnp.logical_not(relay_at(end)))

                @pl.when(waiting)
                def _():
                    in_copy(1, source, step).wait_recv()

            weight_copy(i, j).wait()
            block = rows_in[:, step].reshape(n_t * ROWS, wide)
            acc[...] += lax.dot_general(
                block, weights[j], NT, preferred_element_type=jnp.float32
            )

    bias = bias_ref[...].astype(jnp.float32).reshape(1, acc.shape[1])
    multiply(0, up, jnp.broadcast_to(bias, acc.shape))
    slopes[...] = gelu_slope(acc[...])
    multiply(1, down, jnp.zeros(acc.shape, jnp.float32))
    pre_grad[...] = (slopes[...] * acc[...]).astype(jnp.bfloat16)

    def term_copy(k, c, source):
        dest = lax.rem(t + k, n_t)
        return pltpu.make_async_remote_copy(
            src_ref=terms.at[c, dest], dst_ref=taken.at[source, c],
            send_sem=term_send.at[k - 1, c], recv_sem=term_recv.at[source, c],
            device_id={"tensor": dest}, device_id_type=MESH,
        )

    @pl.loop(0, groups)
    def _(j):
        for s in range(per_group):
            c = j * per_group + s
            term = jnp.dot(
                pre_grad[...], up[j, :, s * COLS : (s + 1) * COLS],
                preferred_element_type=jnp.float32,
            )
            terms[c] = term.astype(jnp.bfloat16).reshape(n_t, ROWS, COLS)
            for k in range(1, n_t):
                term_copy(k, c, t).start()

    for j in range(groups):
        for s in range(per_group):
            c = j * per_group + s
            total = terms[c, t].astype(jnp.float32)
            for k in range(1, n_t):
                source = lax.rem(t + n_t - k, n_t)
                term_copy(k, c, source).wait_recv()
                total = total + taken[source, c].astype(jnp.float32)
            branch[:, c * COLS : (c + 1) * COLS] = total.astype(jnp.bfloat16)
        for side in range(2):
            first = (BAL - halo) if side else 0
            packed = jnp.zeros((ROWS, narrow), jnp.float32)
            for q in range(groups):
                picked = one_hot(
                    (ROWS, ROWS), lambda r, p: (r // halo == q) & (p == first + r % halo)
                )
                start = j * wide + q * narrow
                packed = packed + place(picked, branch[:, start : start + narrow])
            back_out[side, j] = packed.astype(jnp.bfloat16)
            back_copy(side, j).start()

    own_back = one_hot((kmax, ROWS), lambda k, p: p == k + excess)
    live = lax.broadcasted_iota(jnp.int32, (kmax, narrow), 0) < here
    left_back, right_back = [], []
    for q in range(groups):
        left_back.append(one_hot(
            (kmax, ROWS), lambda k, r: (r == q * halo + halo + excess + k) & (k + excess < 0)
        ))
        right_back.append(one_hot(
            (kmax, ROWS),
            lambda k, r: (r == q * halo + excess + k - BAL)
            & (k + excess >= BAL) & (k + excess < BAL + halo),
        ))
    for j in range(groups):
        for side in range(2):
            back_copy(side, j).wait_recv()
        for q in range(groups):
            start = j * wide + q * narrow
            cols = slice(start, start + narrow)
            got = (
                place(own_back, branch[:, cols])
                + place(left_back[q], back_in[0, j])
                + place(right_back[q], back_in[1, j])
            )
            summed = g_ref[:, cols].astype(jnp.float32) + got
            out_ref[:, cols] = jnp.where(live, summed, 0.0).astype(jnp.bfloat16)

    for k in range(1, n_dp):
        count_copy(k, me).wait_send()
    for side in range(2):
        for i in range(2):
            halo_copy(side, i).wait_send()
        for j in range(groups):
            back_copy(side, j).wait_send()

    @pl.loop(0, steps)
    def _(step):
        for k in range(1, n_t):
            @pl.when(sends(k))
            def _():
                in_copy(k, t, step).wait_send()

        for source in relays:
            @pl.when(relay_at(source))
            def _():
                relay_copy(source, step).wait_send()

    @pl.loop(0, chunks)
    def _(c):
        for k in range(1, n_t):
            term_copy(k, c, t).wait_send()


def fused(kept_input, kept_grad, up_weight_t, up_bias, down_weight, kept_count):
    n_dp, n_t = lax.axis_size("dp"), lax.axis_size("tensor")
    kmax, width = kept_input.shape
    hidden = up_weight_t.shape[0]
    chunks = width // COLS
    groups = ROWS // (BAL // 4)
    wide = width // groups
    narrow = wide // groups
    steps = 2 * groups
    tokens = n_t * ROWS
    bf16, f32 = jnp.bfloat16, jnp.float32
    vmem = pl.BlockSpec(memory_space=pltpu.VMEM)
    smem = pl.BlockSpec(memory_space=pltpu.SMEM)
    hbm = pl.BlockSpec(memory_space=pl.ANY)
    dma = pltpu.SemaphoreType.DMA
    return pl.pallas_call(
        functools.partial(fused_kernel, n_dp, n_t),
        out_shape=jax.ShapeDtypeStruct((kmax, width), bf16),
        in_specs=[vmem, vmem, smem, vmem, hbm, hbm],
        out_specs=vmem,
        scratch_shapes=[
            pltpu.VMEM((groups, hidden, wide), bf16),
            pltpu.VMEM((groups, hidden, wide), bf16),
            pltpu.VMEM((n_t, steps, ROWS, wide), bf16),
            pltpu.VMEM((chunks, n_t, ROWS, COLS), bf16),
            pltpu.VMEM((n_t, chunks, ROWS, COLS), bf16),
            pltpu.VMEM((ROWS, width), bf16),
            pltpu.VMEM((tokens, hidden), f32),
            pltpu.VMEM((tokens, hidden), f32),
            pltpu.VMEM((tokens, hidden), bf16),
            pltpu.VMEM((8, 128), jnp.int32),
            pltpu.VMEM((n_dp, 8, 128), jnp.int32),
            pltpu.VMEM((2, 2, ROWS, wide), bf16),
            pltpu.VMEM((2, 2, ROWS, wide), bf16),
            pltpu.VMEM((2, groups, ROWS, narrow), bf16),
            pltpu.VMEM((2, groups, ROWS, narrow), bf16),
            dma((2, groups)),
            dma((n_dp - 1,)),
            dma((n_dp,)),
            dma((2, 2)),
            dma((2, 2)),
            dma((2, groups)),
            dma((2, groups)),
            dma((n_t - 1, steps)),
            dma((n_t, steps)),
            dma((2, steps)),
            dma((n_t - 1, chunks)),
            dma((n_t, chunks)),
        ],
        compiler_params=pltpu.CompilerParams(
            collective_id=0, has_side_effects=True, vmem_limit_bytes=VMEM_LIMIT
        ),
    )(kept_input, kept_grad, kept_count, up_bias, up_weight_t, down_weight)


def fits(mesh, kept_input, up_weight_t):
    hidden = up_weight_t.shape[0] // mesh.shape["tensor"]
    width = up_weight_t.shape[1]
    weights = 2 * hidden * width * 2
    return (
        hidden % ROWS == 0
        and width % (COLS * 4) == 0
        and BAL == ROWS
        and mesh.shape["dp"] > 1
        and mesh.shape["tensor"] > 1
        and weights < VMEM_LIMIT * 3 // 4
    )


def solution(mesh):
    rows = P(("dp", "tensor"), None)
    placed = (rows, rows, P("tensor", None), P("tensor"), P("tensor", None), P(("dp", "tensor")))

    def run(kept_input, kept_grad, up_weight_t, up_bias, down_weight, kept_count):
        chosen = fused if fits(mesh, kept_input, up_weight_t) else body
        return jax.shard_map(
            chosen, mesh=mesh, in_specs=placed, out_specs=rows, check_vma=False
        )(kept_input, kept_grad, up_weight_t, up_bias, down_weight, kept_count)

    return run
```

```python
import functools

import jax
import jax.numpy as jnp
from jax import lax
from jax.experimental import pallas as pl
from jax.experimental.pallas import tpu as pltpu
from jax.sharding import PartitionSpec as P

BAL = 16


INV_SQRT_TWO = 0.7071067811865476
INV_SQRT_TWO_PI = 0.3989422804014327


def prefix(shard, axis, combine, identity):
    length, index = (lax.axis_size(axis), lax.axis_index(axis))
    everything = lax.all_gather(shard, axis)
    start = jnp.broadcast_to(jnp.asarray(identity, shard.dtype), shard.shape)

    def lap(k, before):
        reached = k < index
        new = combine(before, everything[k])
        return jnp.where(reached, new, before)

    return lax.fori_loop(0, length, lap, start)


def padded(block, sides, width):
    for axis, dim in sides:
        count = lax.axis_size(axis)
        forward = [(i, i + 1) for i in range(count - 1)]
        backward = [(target, source) for source, target in forward]
        low = lax.ppermute(
            lax.slice_in_dim(block, block.shape[dim] - width, None, axis=dim), axis, forward
        )
        high = lax.ppermute(lax.slice_in_dim(block, 0, width, axis=dim), axis, backward)
        block = jnp.concatenate([low, block, high], axis=dim)
    return block


def gelu_slope(values):
    return (
        0.5 * (1.0 + lax.erf(values * INV_SQRT_TWO))
        + values * jnp.exp(-0.5 * values * values) * INV_SQRT_TWO_PI
    )


def add_counts(earlier, later):
    return earlier + later


def ffn_rows(stacked, up_weight_t, up_bias, down_weight):
    contract = (((1,), (1,)), ((), ()))
    bias_wide = up_bias.astype(jnp.float32)
    piece_rows = lax.all_gather(stacked, "tensor", axis=0, tiled=True)
    inputs = piece_rows[:, 0]
    out_grads = piece_rows[:, 1]
    preact = (
        lax.dot_general(inputs, up_weight_t, contract, preferred_element_type=jnp.float32)
        + bias_wide
    )
    down_grad = lax.dot_general(
        out_grads, down_weight, contract, preferred_element_type=jnp.float32
    )
    pre_grad = (gelu_slope(preact) * down_grad).astype(jnp.bfloat16)
    partials = jnp.dot(pre_grad, up_weight_t, preferred_element_type=jnp.float32)
    return lax.psum_scatter(
        partials.astype(jnp.bfloat16), "tensor", scatter_dimension=0, tiled=True
    )


def body(kept_input, kept_grad, up_weight_t, up_bias, down_weight, kept_count):
    kmax = kept_input.shape[0]
    count_here = kept_count[0]
    entries = jnp.arange(kmax, dtype=jnp.int32)
    usable = entries < count_here
    stacked = jnp.stack((kept_input, kept_grad), axis=1)
    stacked = jnp.where(usable[:, None, None], stacked, jnp.zeros_like(stacked))
    halo_width = BAL // 4
    spots = BAL + 2 * halo_width
    first_slot = prefix(count_here, "dp", add_counts, jnp.int32(0))
    excess = first_slot - lax.axis_index("dp") * BAL
    target = excess + entries + halo_width
    placing = (target[None, :] == jnp.arange(spots, dtype=jnp.int32)[:, None]) & usable[None, :]
    placing_mat = placing.astype(jnp.bfloat16)
    outgoing = jnp.einsum(
        "sk,kcd->scd", placing_mat, stacked, preferred_element_type=jnp.float32
    ).astype(jnp.bfloat16)
    widened = padded(outgoing, (("dp", 0),), halo_width)
    owned = outgoing[halo_width : halo_width + BAL].astype(jnp.float32)
    owned = owned.at[:halo_width].add(widened[:halo_width].astype(jnp.float32))
    owned = owned.at[BAL - halo_width :].add(
        widened[widened.shape[0] - halo_width :].astype(jnp.float32)
    )
    branch = ffn_rows(owned.astype(jnp.bfloat16), up_weight_t, up_bias, down_weight)
    returned = padded(branch, (("dp", 0),), halo_width)
    own_branch = jnp.einsum(
        "sk,sd->kd", placing_mat, returned, preferred_element_type=jnp.float32
    ).astype(jnp.bfloat16)
    summed = kept_grad.astype(jnp.float32) + own_branch.astype(jnp.float32)
    return jnp.where(usable[:, None], summed, jnp.float32(0.0)).astype(jnp.bfloat16)


ROWS = 16
COLS = 512
LEAD = 3
VMEM_LIMIT = 58 * 1024 * 1024
MESH = pl.DeviceIdType.MESH
NT = (((1,), (1,)), ((), ()))


def one_hot(shape, picked):
    rows = lax.broadcasted_iota(jnp.int32, shape, 0)
    cols = lax.broadcasted_iota(jnp.int32, shape, 1)
    return picked(rows, cols).astype(jnp.float32).astype(jnp.bfloat16)


def place(matrix, block):
    return jnp.dot(matrix, block, preferred_element_type=jnp.float32)


def fused_kernel(
    n_dp, n_t, x_ref, g_ref, count_ref, bias_ref, up_hbm, down_hbm, out_ref,
    up, down, rows_in, terms, taken, passing, branch, acc, slopes, pre_grad,
    count_own, counts, halo_out, halo_in, back_out, back_in,
    w_sem, count_send, count_recv, halo_send, halo_recv, back_send, back_recv,
    in_send, in_recv, relay_send, term_send, term_recv, pass_recv,
):
    me = lax.axis_index("dp")
    t = lax.axis_index("tensor")
    kmax, width = x_ref.shape
    halo = BAL // 4
    groups = ROWS // halo
    wide = width // groups
    narrow = wide // groups
    per_group = wide // COLS
    chunks = width // COLS
    steps = 2 * groups
    left = lax.rem(me + n_dp - 1, n_dp)
    right = lax.rem(me + 1, n_dp)

    def weight_copy(i, j):
        source, target = ((up_hbm, up), (down_hbm, down))[i]
        cols = pl.ds(pl.multiple_of(j * wide, wide), wide)
        return pltpu.make_async_copy(source.at[:, cols], target.at[j], w_sem.at[i, j])

    for i in range(2):
        for j in range(groups):
            weight_copy(i, j).start()

    barrier = pltpu.get_barrier_semaphore()
    for k in range(1, n_dp):
        pl.semaphore_signal(
            barrier, inc=1, device_id={"dp": lax.rem(me + k, n_dp)}, device_id_type=MESH
        )
    for k in range(1, n_t):
        pl.semaphore_signal(
            barrier, inc=1, device_id={"tensor": lax.rem(t + k, n_t)}, device_id_type=MESH
        )

    here = count_ref[0]
    count_own[...] = jnp.full(count_own.shape, here, jnp.int32)
    for side in range(2):
        first = (here - halo) if side else 0
        for i, ref in enumerate((x_ref, g_ref)):
            packed = jnp.zeros((ROWS, wide), jnp.float32)
            for j in range(groups):
                picked = one_hot(
                    (ROWS, kmax), lambda r, k: (r // halo == j) & (k == first + r % halo)
                )
                packed = packed + place(picked, ref[:, j * wide : (j + 1) * wide])
            halo_out[side, i] = packed.astype(jnp.bfloat16)
    pl.semaphore_wait(barrier, n_dp - 1 + n_t - 1)

    def count_copy(k, source):
        return pltpu.make_async_remote_copy(
            src_ref=count_own, dst_ref=counts.at[source],
            send_sem=count_send.at[k - 1], recv_sem=count_recv.at[source],
            device_id={"dp": lax.rem(me + k, n_dp)}, device_id_type=MESH,
        )

    def halo_copy(side, i):
        return pltpu.make_async_remote_copy(
            src_ref=halo_out.at[side, i], dst_ref=halo_in.at[1 - side, i],
            send_sem=halo_send.at[side, i], recv_sem=halo_recv.at[1 - side, i],
            device_id={"dp": right if side else left}, device_id_type=MESH,
        )

    def back_copy(side, j):
        return pltpu.make_async_remote_copy(
            src_ref=back_out.at[side, j], dst_ref=back_in.at[1 - side, j],
            send_sem=back_send.at[side, j], recv_sem=back_recv.at[1 - side, j],
            device_id={"dp": right if side else left}, device_id_type=MESH,
        )

    for k in range(1, n_dp):
        count_copy(k, me).start()
    for i in range(2):
        for side in range(2):
            halo_copy(side, i).start()
    for k in range(1, n_dp):
        count_copy(k, lax.rem(me + n_dp - k, n_dp)).wait_recv()
    before = jnp.zeros(count_own.shape, jnp.int32)
    for j in range(n_dp):
        before = before + jnp.where(j < me, counts[j], 0)
    excess = (before - me * BAL)[0:1, 0:1]
    following = excess + here - BAL

    def in_copy(k, source, step):
        return pltpu.make_async_remote_copy(
            src_ref=rows_in.at[source, step], dst_ref=rows_in.at[source, step],
            send_sem=in_send.at[k - 1, step], recv_sem=in_recv.at[source, step],
            device_id={"tensor": lax.rem(t + k, n_t)}, device_id_type=MESH,
        )

    def relay_copy(source, step):
        return pltpu.make_async_remote_copy(
            src_ref=rows_in.at[source, step], dst_ref=rows_in.at[source, step],
            send_sem=relay_send.at[0 if source else 1, step],
            recv_sem=in_recv.at[source, step],
            device_id={"tensor": n_t - 1 - source}, device_id_type=MESH,
        )

    relays = (0, n_t - 1) if n_t > 2 else ()

    def relay_at(source):
        return t == (1 if source else n_t - 2)

    def sends(k):
        dest = lax.rem(t + k, n_t)
        return jnp.abs(dest - t) < n_t - (1 if relays else 0)

    def start_own(step):
        for k in range(1, n_t):
            @pl.when(sends(k))
            def _():
                in_copy(k, t, step).start()

    own_at = one_hot((ROWS, kmax), lambda p, k: (k == p - excess) & (k < here))
    from_left, from_right = [], []
    for j in range(groups):
        from_left.append(one_hot(
            (ROWS, ROWS), lambda p, r: (r == j * halo + halo - excess + p) & (p < excess)
        ))
        from_right.append(one_hot(
            (ROWS, ROWS),
            lambda p, r: (r == j * halo + p - BAL - following) & (p >= BAL + following),
        ))
    for i, ref in enumerate((x_ref, g_ref)):
        for side in range(2):
            halo_copy(side, i).wait_recv()
        for j in range(groups):
            rows_in[t, i * groups + j] = (
                place(own_at, ref[:, j * wide : (j + 1) * wide])
                + place(from_left[j], halo_in[0, i])
                + place(from_right[j], halo_in[1, i])
            ).astype(jnp.bfloat16)
            if i * groups + j < LEAD:
                start_own(i * groups + j)

    def multiply(i, weights, first):
        acc[...] = first

        @pl.loop(0, groups)
        def _(j):
            step = i * groups + j
            for source in relays:
                @pl.when(relay_at(source))
                def _():
                    in_copy(1, source, step).wait_recv()
                    relay_copy(source, step).start()

            @pl.when(step + LEAD < steps)
            def _():
                start_own(step + LEAD)

            for k in range(1, n_t):
                source = lax.rem(t + n_t - k, n_t)
                waiting = k > 0
                for end in relays:
                    waiting = waiting & ((source != end) | jnp.logical_not(relay_at(end)))

                @pl.when(waiting)
                def _():
                    in_copy(1, source, step).wait_recv()

            weight_copy(i, j).wait()
            block = rows_in[:, step].reshape(n_t * ROWS, wide)
            acc[...] += lax.dot_general(
                block, weights[j], NT, preferred_element_type=jnp.float32
            )

    bias = bias_ref[...].astype(jnp.float32).reshape(1, acc.shape[1])
    multiply(0, up, jnp.broadcast_to(bias, acc.shape))
    slopes[...] = gelu_slope(acc[...])
    multiply(1, down, jnp.zeros(acc.shape, jnp.float32))
    pre_grad[...] = (slopes[...] * acc[...]).astype(jnp.bfloat16)

    def term_copy(k, c, source):
        dest = lax.rem(t + k, n_t)
        return pltpu.make_async_remote_copy(
            src_ref=terms.at[c, dest], dst_ref=taken.at[source, c],
            send_sem=term_send.at[k - 1, c], recv_sem=term_recv.at[source, c],
            device_id={"tensor": dest}, device_id_type=MESH,
        )

    def far_copy(k, end, c):
        return pltpu.make_async_remote_copy(
            src_ref=terms.at[c, end], dst_ref=passing.at[0 if end else 1, c],
            send_sem=term_send.at[k - 1, c], recv_sem=pass_recv.at[0 if end else 1, c],
            device_id={"tensor": 1 if end else n_t - 2}, device_id_type=MESH,
        )

    def adds_for(end):
        return t == (1 if end else n_t - 2)

    def start_terms(c):
        for end in relays:
            @pl.when(t == n_t - 1 - end)
            def _():
                far_copy(n_t - 1 if end else 1, end, c).start()
        for k in range(1, n_t):
            dest = lax.rem(t + k, n_t)
            direct = sends(k)
            for end in relays:
                direct = direct & ((dest != end) | jnp.logical_not(adds_for(end)))

            @pl.when(direct)
            def _():
                term_copy(k, c, t).start()

    def start_sums(c):
        for end in relays:
            @pl.when(adds_for(end))
            def _():
                k = n_t - 2 if end else 2
                far_copy(1, end, c).wait_recv()
                both = terms[c, end].astype(jnp.float32) + passing[
                    0 if end else 1, c
                ].astype(jnp.float32)
                terms[c, end] = both.astype(jnp.bfloat16)
                term_copy(k, c, t).start()

    @pl.loop(0, groups)
    def _(j):
        for s in range(per_group):
            c = j * per_group + s
            term = jnp.dot(
                pre_grad[...], up[j, :, s * COLS : (s + 1) * COLS],
                preferred_element_type=jnp.float32,
            )
            terms[c] = term.astype(jnp.bfloat16).reshape(n_t, ROWS, COLS)
            start_terms(c)

        @pl.when(j > 0)
        def _():
            for s in range(per_group):
                start_sums((j - 1) * per_group + s)

    for s in range(per_group):
        start_sums((groups - 1) * per_group + s)

    for j in range(groups):
        for s in range(per_group):
            c = j * per_group + s
            total = terms[c, t].astype(jnp.float32)
            for k in range(1, n_t):
                source = lax.rem(t + n_t - k, n_t)
                comes = sends(n_t - k)

                @pl.when(comes)
                def _():
                    term_copy(k, c, source).wait_recv()

                @pl.when(jnp.logical_not(comes))
                def _():
                    taken[source, c] = jnp.zeros((ROWS, COLS), jnp.bfloat16)

                total = total + taken[source, c].astype(jnp.float32)
            branch[:, c * COLS : (c + 1) * COLS] = total.astype(jnp.bfloat16)
        for side in range(2):
            first = (BAL - halo) if side else 0
            packed = jnp.zeros((ROWS, narrow), jnp.float32)
            for q in range(groups):
                picked = one_hot(
                    (ROWS, ROWS), lambda r, p: (r // halo == q) & (p == first + r % halo)
                )
                start = j * wide + q * narrow
                packed = packed + place(picked, branch[:, start : start + narrow])
            back_out[side, j] = packed.astype(jnp.bfloat16)
            back_copy(side, j).start()

    own_back = one_hot((kmax, ROWS), lambda k, p: p == k + excess)
    live = lax.broadcasted_iota(jnp.int32, (kmax, narrow), 0) < here
    left_back, right_back = [], []
    for q in range(groups):
        left_back.append(one_hot(
            (kmax, ROWS), lambda k, r: (r == q * halo + halo + excess + k) & (k + excess < 0)
        ))
        right_back.append(one_hot(
            (kmax, ROWS),
            lambda k, r: (r == q * halo + excess + k - BAL)
            & (k + excess >= BAL) & (k + excess < BAL + halo),
        ))
    for j in range(groups):
        for side in range(2):
            back_copy(side, j).wait_recv()
        for q in range(groups):
            start = j * wide + q * narrow
            cols = slice(start, start + narrow)
            got = (
                place(own_back, branch[:, cols])
                + place(left_back[q], back_in[0, j])
                + place(right_back[q], back_in[1, j])
            )
            summed = g_ref[:, cols].astype(jnp.float32) + got
            out_ref[:, cols] = jnp.where(live, summed, 0.0).astype(jnp.bfloat16)

    for k in range(1, n_dp):
        count_copy(k, me).wait_send()
    for side in range(2):
        for i in range(2):
            halo_copy(side, i).wait_send()
        for j in range(groups):
            back_copy(side, j).wait_send()

    @pl.loop(0, steps)
    def _(step):
        for k in range(1, n_t):
            @pl.when(sends(k))
            def _():
                in_copy(k, t, step).wait_send()

        for source in relays:
            @pl.when(relay_at(source))
            def _():
                relay_copy(source, step).wait_send()

    @pl.loop(0, chunks)
    def _(c):
        for k in range(1, n_t):
            term_copy(k, c, t).wait_send()


def fused(kept_input, kept_grad, up_weight_t, up_bias, down_weight, kept_count):
    n_dp, n_t = lax.axis_size("dp"), lax.axis_size("tensor")
    kmax, width = kept_input.shape
    hidden = up_weight_t.shape[0]
    chunks = width // COLS
    groups = ROWS // (BAL // 4)
    wide = width // groups
    narrow = wide // groups
    steps = 2 * groups
    tokens = n_t * ROWS
    bf16, f32 = jnp.bfloat16, jnp.float32
    vmem = pl.BlockSpec(memory_space=pltpu.VMEM)
    smem = pl.BlockSpec(memory_space=pltpu.SMEM)
    hbm = pl.BlockSpec(memory_space=pl.ANY)
    dma = pltpu.SemaphoreType.DMA
    return pl.pallas_call(
        functools.partial(fused_kernel, n_dp, n_t),
        out_shape=jax.ShapeDtypeStruct((kmax, width), bf16),
        in_specs=[vmem, vmem, smem, vmem, hbm, hbm],
        out_specs=vmem,
        scratch_shapes=[
            pltpu.VMEM((groups, hidden, wide), bf16),
            pltpu.VMEM((groups, hidden, wide), bf16),
            pltpu.VMEM((n_t, steps, ROWS, wide), bf16),
            pltpu.VMEM((chunks, n_t, ROWS, COLS), bf16),
            pltpu.VMEM((n_t, chunks, ROWS, COLS), bf16),
            pltpu.VMEM((2, chunks, ROWS, COLS), bf16),
            pltpu.VMEM((ROWS, width), bf16),
            pltpu.VMEM((tokens, hidden), f32),
            pltpu.VMEM((tokens, hidden), f32),
            pltpu.VMEM((tokens, hidden), bf16),
            pltpu.VMEM((8, 128), jnp.int32),
            pltpu.VMEM((n_dp, 8, 128), jnp.int32),
            pltpu.VMEM((2, 2, ROWS, wide), bf16),
            pltpu.VMEM((2, 2, ROWS, wide), bf16),
            pltpu.VMEM((2, groups, ROWS, narrow), bf16),
            pltpu.VMEM((2, groups, ROWS, narrow), bf16),
            dma((2, groups)),
            dma((n_dp - 1,)),
            dma((n_dp,)),
            dma((2, 2)),
            dma((2, 2)),
            dma((2, groups)),
            dma((2, groups)),
            dma((n_t - 1, steps)),
            dma((n_t, steps)),
            dma((2, steps)),
            dma((n_t - 1, chunks)),
            dma((n_t, chunks)),
            dma((2, chunks)),
        ],
        compiler_params=pltpu.CompilerParams(
            collective_id=0, has_side_effects=True, vmem_limit_bytes=VMEM_LIMIT
        ),
    )(kept_input, kept_grad, kept_count, up_bias, up_weight_t, down_weight)


def fits(mesh, kept_input, up_weight_t):
    hidden = up_weight_t.shape[0] // mesh.shape["tensor"]
    width = up_weight_t.shape[1]
    weights = 2 * hidden * width * 2
    return (
        hidden % ROWS == 0
        and width % (COLS * 4) == 0
        and BAL == ROWS
        and mesh.shape["dp"] > 1
        and mesh.shape["tensor"] > 1
        and weights < VMEM_LIMIT * 3 // 4
    )


def solution(mesh):
    rows = P(("dp", "tensor"), None)
    placed = (rows, rows, P("tensor", None), P("tensor"), P("tensor", None), P(("dp", "tensor")))

    def run(kept_input, kept_grad, up_weight_t, up_bias, down_weight, kept_count):
        chosen = fused if fits(mesh, kept_input, up_weight_t) else body
        return jax.shard_map(
            chosen, mesh=mesh, in_specs=placed, out_specs=rows, check_vma=False
        )(kept_input, kept_grad, up_weight_t, up_bias, down_weight, kept_count)

    return run
```

```python
import functools

import jax
import jax.numpy as jnp
from jax import lax
from jax.experimental import pallas as pl
from jax.experimental.pallas import tpu as pltpu
from jax.sharding import PartitionSpec as P

BAL = 16


INV_SQRT_TWO = 0.7071067811865476
INV_SQRT_TWO_PI = 0.3989422804014327


def prefix(shard, axis, combine, identity):
    length, index = (lax.axis_size(axis), lax.axis_index(axis))
    everything = lax.all_gather(shard, axis)
    start = jnp.broadcast_to(jnp.asarray(identity, shard.dtype), shard.shape)

    def lap(k, before):
        reached = k < index
        new = combine(before, everything[k])
        return jnp.where(reached, new, before)

    return lax.fori_loop(0, length, lap, start)


def padded(block, sides, width):
    for axis, dim in sides:
        count = lax.axis_size(axis)
        forward = [(i, i + 1) for i in range(count - 1)]
        backward = [(target, source) for source, target in forward]
        low = lax.ppermute(
            lax.slice_in_dim(block, block.shape[dim] - width, None, axis=dim), axis, forward
        )
        high = lax.ppermute(lax.slice_in_dim(block, 0, width, axis=dim), axis, backward)
        block = jnp.concatenate([low, block, high], axis=dim)
    return block


def gelu_slope(values):
    return (
        0.5 * (1.0 + lax.erf(values * INV_SQRT_TWO))
        + values * jnp.exp(-0.5 * values * values) * INV_SQRT_TWO_PI
    )


def add_counts(earlier, later):
    return earlier + later


def ffn_rows(stacked, up_weight_t, up_bias, down_weight):
    contract = (((1,), (1,)), ((), ()))
    bias_wide = up_bias.astype(jnp.float32)
    piece_rows = lax.all_gather(stacked, "tensor", axis=0, tiled=True)
    inputs = piece_rows[:, 0]
    out_grads = piece_rows[:, 1]
    preact = (
        lax.dot_general(inputs, up_weight_t, contract, preferred_element_type=jnp.float32)
        + bias_wide
    )
    down_grad = lax.dot_general(
        out_grads, down_weight, contract, preferred_element_type=jnp.float32
    )
    pre_grad = (gelu_slope(preact) * down_grad).astype(jnp.bfloat16)
    partials = jnp.dot(pre_grad, up_weight_t, preferred_element_type=jnp.float32)
    return lax.psum_scatter(
        partials.astype(jnp.bfloat16), "tensor", scatter_dimension=0, tiled=True
    )


def body(kept_input, kept_grad, up_weight_t, up_bias, down_weight, kept_count):
    kmax = kept_input.shape[0]
    count_here = kept_count[0]
    entries = jnp.arange(kmax, dtype=jnp.int32)
    usable = entries < count_here
    stacked = jnp.stack((kept_input, kept_grad), axis=1)
    stacked = jnp.where(usable[:, None, None], stacked, jnp.zeros_like(stacked))
    halo_width = BAL // 4
    spots = BAL + 2 * halo_width
    first_slot = prefix(count_here, "dp", add_counts, jnp.int32(0))
    excess = first_slot - lax.axis_index("dp") * BAL
    target = excess + entries + halo_width
    placing = (target[None, :] == jnp.arange(spots, dtype=jnp.int32)[:, None]) & usable[None, :]
    placing_mat = placing.astype(jnp.bfloat16)
    outgoing = jnp.einsum(
        "sk,kcd->scd", placing_mat, stacked, preferred_element_type=jnp.float32
    ).astype(jnp.bfloat16)
    widened = padded(outgoing, (("dp", 0),), halo_width)
    owned = outgoing[halo_width : halo_width + BAL].astype(jnp.float32)
    owned = owned.at[:halo_width].add(widened[:halo_width].astype(jnp.float32))
    owned = owned.at[BAL - halo_width :].add(
        widened[widened.shape[0] - halo_width :].astype(jnp.float32)
    )
    branch = ffn_rows(owned.astype(jnp.bfloat16), up_weight_t, up_bias, down_weight)
    returned = padded(branch, (("dp", 0),), halo_width)
    own_branch = jnp.einsum(
        "sk,sd->kd", placing_mat, returned, preferred_element_type=jnp.float32
    ).astype(jnp.bfloat16)
    summed = kept_grad.astype(jnp.float32) + own_branch.astype(jnp.float32)
    return jnp.where(usable[:, None], summed, jnp.float32(0.0)).astype(jnp.bfloat16)


ROWS = 16
COLS = 512
LEAD = 3
VMEM_LIMIT = 58 * 1024 * 1024
MESH = pl.DeviceIdType.MESH
NT = (((1,), (1,)), ((), ()))


def one_hot(shape, picked):
    rows = lax.broadcasted_iota(jnp.int32, shape, 0)
    cols = lax.broadcasted_iota(jnp.int32, shape, 1)
    return picked(rows, cols).astype(jnp.float32).astype(jnp.bfloat16)


def place(matrix, block):
    return jnp.dot(matrix, block, preferred_element_type=jnp.float32)


def fused_kernel(
    n_dp, n_t, x_ref, g_ref, count_ref, bias_ref, up_hbm, down_hbm, out_ref,
    up, down, rows_in, terms, taken, branch, acc, slopes, pre_grad,
    count_own, counts, halo_out, halo_in, back_out, back_in,
    w_sem, count_send, count_recv, halo_send, halo_recv, back_send, back_recv,
    in_send, in_recv, relay_send, term_send, term_recv,
):
    me = lax.axis_index("dp")
    t = lax.axis_index("tensor")
    kmax, width = x_ref.shape
    halo = BAL // 4
    groups = ROWS // halo
    wide = width // groups
    narrow = wide // groups
    per_group = wide // COLS
    chunks = width // COLS
    steps = 2 * groups
    left = lax.rem(me + n_dp - 1, n_dp)
    right = lax.rem(me + 1, n_dp)

    def weight_copy(i, j):
        source, target = ((up_hbm, up), (down_hbm, down))[i]
        cols = pl.ds(pl.multiple_of(j * wide, wide), wide)
        return pltpu.make_async_copy(source.at[:, cols], target.at[j], w_sem.at[i, j])

    for j in range(groups // 2):
        weight_copy(0, j).start()

    barrier = pltpu.get_barrier_semaphore()
    for k in range(1, n_dp):
        pl.semaphore_signal(
            barrier, inc=1, device_id={"dp": lax.rem(me + k, n_dp)}, device_id_type=MESH
        )
    for k in range(1, n_t):
        pl.semaphore_signal(
            barrier, inc=1, device_id={"tensor": lax.rem(t + k, n_t)}, device_id_type=MESH
        )

    here = count_ref[0]
    count_own[...] = jnp.full(count_own.shape, here, jnp.int32)
    for side in range(2):
        first = (here - halo) if side else 0
        for i, ref in enumerate((x_ref, g_ref)):
            packed = jnp.zeros((ROWS, wide), jnp.float32)
            for j in range(groups):
                picked = one_hot(
                    (ROWS, kmax), lambda r, k: (r // halo == j) & (k == first + r % halo)
                )
                packed = packed + place(picked, ref[:, j * wide : (j + 1) * wide])
            halo_out[side, i] = packed.astype(jnp.bfloat16)
    pl.semaphore_wait(barrier, n_dp - 1 + n_t - 1)

    def count_copy(k, source):
        return pltpu.make_async_remote_copy(
            src_ref=count_own, dst_ref=counts.at[source],
            send_sem=count_send.at[k - 1], recv_sem=count_recv.at[source],
            device_id={"dp": lax.rem(me + k, n_dp)}, device_id_type=MESH,
        )

    def halo_copy(side, i):
        return pltpu.make_async_remote_copy(
            src_ref=halo_out.at[side, i], dst_ref=halo_in.at[1 - side, i],
            send_sem=halo_send.at[side, i], recv_sem=halo_recv.at[1 - side, i],
            device_id={"dp": right if side else left}, device_id_type=MESH,
        )

    def back_copy(side, j):
        return pltpu.make_async_remote_copy(
            src_ref=back_out.at[side, j], dst_ref=back_in.at[1 - side, j],
            send_sem=back_send.at[side, j], recv_sem=back_recv.at[1 - side, j],
            device_id={"dp": right if side else left}, device_id_type=MESH,
        )

    for k in range(1, n_dp):
        count_copy(k, me).start()
    for i in range(2):
        for side in range(2):
            halo_copy(side, i).start()
    for j in range(groups // 2, groups):
        weight_copy(0, j).start()
    for k in range(1, n_dp):
        count_copy(k, lax.rem(me + n_dp - k, n_dp)).wait_recv()
    before = jnp.zeros(count_own.shape, jnp.int32)
    for j in range(n_dp):
        before = before + jnp.where(j < me, counts[j], 0)
    excess = (before - me * BAL)[0:1, 0:1]
    following = excess + here - BAL

    def in_copy(k, source, step):
        return pltpu.make_async_remote_copy(
            src_ref=rows_in.at[source, step], dst_ref=rows_in.at[source, step],
            send_sem=in_send.at[k - 1, step], recv_sem=in_recv.at[source, step],
            device_id={"tensor": lax.rem(t + k, n_t)}, device_id_type=MESH,
        )

    def relay_copy(source, step):
        return pltpu.make_async_remote_copy(
            src_ref=rows_in.at[source, step], dst_ref=rows_in.at[source, step],
            send_sem=relay_send.at[0 if source else 1, step],
            recv_sem=in_recv.at[source, step],
            device_id={"tensor": n_t - 1 - source}, device_id_type=MESH,
        )

    relays = (0, n_t - 1) if n_t > 2 else ()

    def relay_at(source):
        return t == (1 if source else n_t - 2)

    def sends(k):
        dest = lax.rem(t + k, n_t)
        return jnp.abs(dest - t) < n_t - (1 if relays else 0)

    def start_own(step):
        for k in range(1, n_t):
            @pl.when(sends(k))
            def _():
                in_copy(k, t, step).start()

    own_at = one_hot((ROWS, kmax), lambda p, k: (k == p - excess) & (k < here))
    from_left, from_right = [], []
    for j in range(groups):
        from_left.append(one_hot(
            (ROWS, ROWS), lambda p, r: (r == j * halo + halo - excess + p) & (p < excess)
        ))
        from_right.append(one_hot(
            (ROWS, ROWS),
            lambda p, r: (r == j * halo + p - BAL - following) & (p >= BAL + following),
        ))
    for i, ref in enumerate((x_ref, g_ref)):
        for side in range(2):
            halo_copy(side, i).wait_recv()
        for j in range(groups):
            rows_in[t, i * groups + j] = (
                place(own_at, ref[:, j * wide : (j + 1) * wide])
                + place(from_left[j], halo_in[0, i])
                + place(from_right[j], halo_in[1, i])
            ).astype(jnp.bfloat16)
            if i * groups + j < LEAD:
                start_own(i * groups + j)

    def multiply(i, weights, first):
        acc[...] = first

        @pl.loop(0, groups)
        def _(j):
            step = i * groups + j
            for source in relays:
                @pl.when(relay_at(source))
                def _():
                    in_copy(1, source, step).wait_recv()
                    relay_copy(source, step).start()

            @pl.when(step + LEAD < steps)
            def _():
                start_own(step + LEAD)

            if i == 0:
                weight_copy(1, j).start()

            for k in range(1, n_t):
                source = lax.rem(t + n_t - k, n_t)
                waiting = k > 0
                for end in relays:
                    waiting = waiting & ((source != end) | jnp.logical_not(relay_at(end)))

                @pl.when(waiting)
                def _():
                    in_copy(1, source, step).wait_recv()

            weight_copy(i, j).wait()
            block = rows_in[:, step].reshape(n_t * ROWS, wide)
            acc[...] += lax.dot_general(
                block, weights[j], NT, preferred_element_type=jnp.float32
            )

    bias = bias_ref[...].astype(jnp.float32).reshape(1, acc.shape[1])
    multiply(0, up, jnp.broadcast_to(bias, acc.shape))
    slopes[...] = gelu_slope(acc[...])
    multiply(1, down, jnp.zeros(acc.shape, jnp.float32))
    pre_grad[...] = (slopes[...] * acc[...]).astype(jnp.bfloat16)

    def term_copy(k, c, source):
        dest = lax.rem(t + k, n_t)
        return pltpu.make_async_remote_copy(
            src_ref=terms.at[c, dest], dst_ref=taken.at[source, c],
            send_sem=term_send.at[k - 1, c], recv_sem=term_recv.at[source, c],
            device_id={"tensor": dest}, device_id_type=MESH,
        )

    @pl.loop(0, groups)
    def _(j):
        for s in range(per_group):
            c = j * per_group + s
            term = jnp.dot(
                pre_grad[...], up[j, :, s * COLS : (s + 1) * COLS],
                preferred_element_type=jnp.float32,
            )
            terms[c] = term.astype(jnp.bfloat16).reshape(n_t, ROWS, COLS)
            for k in range(1, n_t):
                term_copy(k, c, t).start()

    for j in range(groups):
        for s in range(per_group):
            c = j * per_group + s
            total = terms[c, t].astype(jnp.float32)
            for k in range(1, n_t):
                source = lax.rem(t + n_t - k, n_t)
                term_copy(k, c, source).wait_recv()
                total = total + taken[source, c].astype(jnp.float32)
            branch[:, c * COLS : (c + 1) * COLS] = total.astype(jnp.bfloat16)
        for side in range(2):
            first = (BAL - halo) if side else 0
            packed = jnp.zeros((ROWS, narrow), jnp.float32)
            for q in range(groups):
                picked = one_hot(
                    (ROWS, ROWS), lambda r, p: (r // halo == q) & (p == first + r % halo)
                )
                start = j * wide + q * narrow
                packed = packed + place(picked, branch[:, start : start + narrow])
            back_out[side, j] = packed.astype(jnp.bfloat16)
            back_copy(side, j).start()

    own_back = one_hot((kmax, ROWS), lambda k, p: p == k + excess)
    live = lax.broadcasted_iota(jnp.int32, (kmax, narrow), 0) < here
    left_back, right_back = [], []
    for q in range(groups):
        left_back.append(one_hot(
            (kmax, ROWS), lambda k, r: (r == q * halo + halo + excess + k) & (k + excess < 0)
        ))
        right_back.append(one_hot(
            (kmax, ROWS),
            lambda k, r: (r == q * halo + excess + k - BAL)
            & (k + excess >= BAL) & (k + excess < BAL + halo),
        ))
    for j in range(groups):
        for side in range(2):
            back_copy(side, j).wait_recv()
        for q in range(groups):
            start = j * wide + q * narrow
            cols = slice(start, start + narrow)
            got = (
                place(own_back, branch[:, cols])
                + place(left_back[q], back_in[0, j])
                + place(right_back[q], back_in[1, j])
            )
            summed = g_ref[:, cols].astype(jnp.float32) + got
            out_ref[:, cols] = jnp.where(live, summed, 0.0).astype(jnp.bfloat16)

    for k in range(1, n_dp):
        count_copy(k, me).wait_send()
    for side in range(2):
        for i in range(2):
            halo_copy(side, i).wait_send()
        for j in range(groups):
            back_copy(side, j).wait_send()

    @pl.loop(0, steps)
    def _(step):
        for k in range(1, n_t):
            @pl.when(sends(k))
            def _():
                in_copy(k, t, step).wait_send()

        for source in relays:
            @pl.when(relay_at(source))
            def _():
                relay_copy(source, step).wait_send()

    @pl.loop(0, chunks)
    def _(c):
        for k in range(1, n_t):
            term_copy(k, c, t).wait_send()


def fused(kept_input, kept_grad, up_weight_t, up_bias, down_weight, kept_count):
    n_dp, n_t = lax.axis_size("dp"), lax.axis_size("tensor")
    kmax, width = kept_input.shape
    hidden = up_weight_t.shape[0]
    chunks = width // COLS
    groups = ROWS // (BAL // 4)
    wide = width // groups
    narrow = wide // groups
    steps = 2 * groups
    tokens = n_t * ROWS
    bf16, f32 = jnp.bfloat16, jnp.float32
    vmem = pl.BlockSpec(memory_space=pltpu.VMEM)
    smem = pl.BlockSpec(memory_space=pltpu.SMEM)
    hbm = pl.BlockSpec(memory_space=pl.ANY)
    dma = pltpu.SemaphoreType.DMA
    return pl.pallas_call(
        functools.partial(fused_kernel, n_dp, n_t),
        out_shape=jax.ShapeDtypeStruct((kmax, width), bf16),
        in_specs=[vmem, vmem, smem, vmem, hbm, hbm],
        out_specs=vmem,
        scratch_shapes=[
            pltpu.VMEM((groups, hidden, wide), bf16),
            pltpu.VMEM((groups, hidden, wide), bf16),
            pltpu.VMEM((n_t, steps, ROWS, wide), bf16),
            pltpu.VMEM((chunks, n_t, ROWS, COLS), bf16),
            pltpu.VMEM((n_t, chunks, ROWS, COLS), bf16),
            pltpu.VMEM((ROWS, width), bf16),
            pltpu.VMEM((tokens, hidden), f32),
            pltpu.VMEM((tokens, hidden), f32),
            pltpu.VMEM((tokens, hidden), bf16),
            pltpu.VMEM((8, 128), jnp.int32),
            pltpu.VMEM((n_dp, 8, 128), jnp.int32),
            pltpu.VMEM((2, 2, ROWS, wide), bf16),
            pltpu.VMEM((2, 2, ROWS, wide), bf16),
            pltpu.VMEM((2, groups, ROWS, narrow), bf16),
            pltpu.VMEM((2, groups, ROWS, narrow), bf16),
            dma((2, groups)),
            dma((n_dp - 1,)),
            dma((n_dp,)),
            dma((2, 2)),
            dma((2, 2)),
            dma((2, groups)),
            dma((2, groups)),
            dma((n_t - 1, steps)),
            dma((n_t, steps)),
            dma((2, steps)),
            dma((n_t - 1, chunks)),
            dma((n_t, chunks)),
        ],
        compiler_params=pltpu.CompilerParams(
            collective_id=0, has_side_effects=True, vmem_limit_bytes=VMEM_LIMIT
        ),
    )(kept_input, kept_grad, kept_count, up_bias, up_weight_t, down_weight)


def fits(mesh, kept_input, up_weight_t):
    hidden = up_weight_t.shape[0] // mesh.shape["tensor"]
    width = up_weight_t.shape[1]
    weights = 2 * hidden * width * 2
    return (
        hidden % ROWS == 0
        and width % (COLS * 4) == 0
        and BAL == ROWS
        and mesh.shape["dp"] > 1
        and mesh.shape["tensor"] > 1
        and weights < VMEM_LIMIT * 3 // 4
    )


def solution(mesh):
    rows = P(("dp", "tensor"), None)
    placed = (rows, rows, P("tensor", None), P("tensor"), P("tensor", None), P(("dp", "tensor")))

    def run(kept_input, kept_grad, up_weight_t, up_bias, down_weight, kept_count):
        chosen = fused if fits(mesh, kept_input, up_weight_t) else body
        return jax.shard_map(
            chosen, mesh=mesh, in_specs=placed, out_specs=rows, check_vma=False
        )(kept_input, kept_grad, up_weight_t, up_bias, down_weight, kept_count)

    return run
```
